32 devices in a mesh: ctx: 8 (over y, x, core), fsdp: 4 (over z).
Axes of the slice: x: 2, y: 2, z: 4, core: 2. Of those that a mesh axis runs over, the one named last changes fastest.
Arguments:
- hidden_in: bfloat16 [2, 8, 1024, 1024], P(None, 'fsdp', 'ctx'), may hold values from -6 to 6
- lengths: int32 [2, 8], P(None, 'fsdp'), may hold values from 256 to 1024, as said below
- cotangent: bfloat16 [2, 8, 1024, 1024], P(None, 'fsdp', 'ctx'), may hold values from -6 to 6
- w_qkv: bfloat16 [1024, 3072], P('fsdp'), may hold values from -0.1875 to 0.1875
- bias_q: bfloat16 [1024], P('fsdp'), may hold values from -3 to 3
- bias_v: bfloat16 [1024], P('fsdp'), may hold values from -0.1875 to 0.1875
- w_out: bfloat16 [1024, 1024], P('fsdp'), may hold values from -4 to 4
- bias_out: bfloat16 [1024], P('fsdp'), may hold values from -2 to 2
- ln1_gain: bfloat16 [1024], P('fsdp'), may hold values from 0.25 to 1.75
- ln1_bias: bfloat16 [1024], P('fsdp'), may hold values from -2 to 2
- w_up: bfloat16 [1024, 4096], P('fsdp'), may hold values from -0.1875 to 0.1875
- bias_up: bfloat16 [4096], P('fsdp'), may hold values from -3 to 3
- w_down: bfloat16 [4096, 1024], P('fsdp'), may hold values from -0.09375 to 0.09375
- bias_down: bfloat16 [1024], P('fsdp'), may hold values from -2 to 2
- ln2_gain: bfloat16 [1024], P('fsdp'), may hold values from 0.25 to 1.75
- ln2_bias: bfloat16 [1024], P('fsdp'), may hold values from -2 to 2
Outputs:
- out_hidden: bfloat16 [2, 8, 1024, 1024], P(None, 'fsdp', 'ctx')
- grad_hidden: float32 [2, 8, 1024, 1024], P(None, 'fsdp', 'ctx')
- grad_w_qkv: float32 [1024, 3072], P('fsdp')
- grad_bias_q: float32 [1024], P('fsdp')
- grad_bias_v: float32 [1024], P('fsdp')
- grad_w_out: float32 [1024, 1024], P('fsdp')
- grad_bias_out: float32 [1024], P('fsdp')
- grad_ln1_gain: float32 [1024], P('fsdp')
- grad_ln1_bias: float32 [1024], P('fsdp')
- grad_w_up: float32 [1024, 4096], P('fsdp')
- grad_bias_up: float32 [4096], P('fsdp')
- grad_w_down: float32 [4096, 1024], P('fsdp')
- grad_bias_down: float32 [1024], P('fsdp')
- grad_ln2_gain: float32 [1024], P('fsdp')
- grad_ln2_bias: float32 [1024], P('fsdp')
The draws below stay inside these ranges and needn't reach their ends.
Inputs may be any that keep to these rules, and one draw needn't show every extreme that they name: `lengths`: in every micro-batch, one of the 2 sequences of each index of fsdp, chosen by the seed, fills all 1024 slots.
All inputs are finite; a program needn't handle non-finite values.
Results may differ from the reference program's by a relative error of at most 0.025.
Values may be sent and summed in bfloat16 or wider, within the bound.
A program may use at most 384 MiB of HBM per device.

```python
import jax
import jax.numpy as jnp
from jax import lax

D = 1024
HEADS = 16
HEAD_DIM = 64
FF = 4096
SEQS = 2
MB = 2
SLOTS = 1024
SEQ_ALL = 8


def draw_lengths(key, part):
    key = jax.random.fold_in(key, 7)
    key_values, key_pick = jax.random.split(key)
    groups = SEQ_ALL // SEQS
    values = jax.random.randint(key_values, (MB, groups, SEQS), SLOTS // 4, SLOTS + 1, dtype=jnp.int32)
    picked = jax.random.randint(key_pick, (MB, groups, 1), 0, SEQS, dtype=jnp.int32)
    chosen = jnp.arange(SEQS, dtype=jnp.int32)[None, None, :] == picked
    values = jnp.where(chosen, SLOTS, values)
    return values.reshape(MB, SEQ_ALL).astype(jnp.int32)


def level_of(rng, extent, pieces, smallest, high):
    loudness = 1.0
    for position, parts in pieces:
        draws = jax.random.uniform(jax.random.fold_in(jax.random.fold_in(rng, 6), position), (parts,), jnp.float32, smallest / len(pieces), high / len(pieces))
        loudness = loudness * jnp.repeat(jnp.exp(draws), extent[position] // parts).reshape((-1,) + (1,) * (len(extent) - 1 - position))
    return loudness


def noise(key, shape, scale, limit, cuts=(), kind=jnp.bfloat16):
    entries = scale * jax.random.normal(key, shape, jnp.float32)
    if cuts:
        entries = entries * level_of(key, shape, cuts, -0.22, 0.18)
    return jnp.clip(entries, -limit, limit).astype(kind)


def setup_inputs(seed: int = 0) -> dict:
    keys = jax.random.split(jax.random.key(seed), 17)
    hidden_in = noise(keys[0], (MB, SEQ_ALL, SLOTS, D), 1.0, 6.0, ((1, 4), (2, 8)))
    lengths = draw_lengths(jax.random.fold_in(keys[16], 71), 0)
    cotangent = noise(keys[2], (MB, SEQ_ALL, SLOTS, D), 1.0, 6.0, ((1, 4), (2, 8)))
    w_qkv = noise(keys[3], (D, 3 * D), D ** -0.5, 0.1875, ((0, 4),))
    bias_q = noise(keys[4], (D,), 0.5, 3.0, ((0, 4),))
    bias_v = noise(keys[5], (D,), D ** -0.5, 0.1875, ((0, 4),))
    w_out = noise(keys[6], (D, D), (max(1, 2 * D // SLOTS)) ** -0.5, 4.0, ((0, 4),))
    bias_out = noise(keys[7], (D,), 0.3, 2.0, ((0, 4),))
    ln1_gain = jnp.clip(1.0 + 0.15 * jax.random.normal(keys[8], (D,), jnp.float32), 0.25, 1.75).astype(jnp.bfloat16)
    ln1_bias = noise(keys[9], (D,), 0.3, 2.0, ((0, 4),))
    w_up = noise(keys[10], (D, FF), D ** -0.5, 0.1875, ((0, 4),))
    bias_up = noise(keys[11], (FF,), 0.5, 3.0, ((0, 4),))
    w_down = noise(keys[12], (FF, D), FF ** -0.5, 0.09375, ((0, 4),))
    bias_down = noise(keys[13], (D,), 0.3, 2.0, ((0, 4),))
    ln2_gain = jnp.clip(1.0 + 0.15 * jax.random.normal(keys[14], (D,), jnp.float32), 0.25, 1.75).astype(jnp.bfloat16)
    ln2_bias = noise(keys[15], (D,), 0.3, 2.0, ((0, 4),))
    return {"hidden_in": hidden_in, "lengths": lengths, "cotangent": cotangent, "w_qkv": w_qkv, "bias_q": bias_q, "bias_v": bias_v, "w_out": w_out, "bias_out": bias_out, "ln1_gain": ln1_gain, "ln1_bias": ln1_bias, "w_up": w_up, "bias_up": bias_up, "w_down": w_down, "bias_down": bias_down, "ln2_gain": ln2_gain, "ln2_bias": ln2_bias}


@jax.custom_vjp
def low(v):
    return lax.optimization_barrier(v.astype(jnp.bfloat16)).astype(jnp.float32)

@jax.custom_vjp
def low_back(v):
    return v

def low_keep(v):
    return (low(v), None)

def low_pass(kept, grad):
    return (grad,)

def back_keep(v):
    return (v, None)

def back_low(kept, grad):
    return (low(grad),)
low.defvjp(low_keep, low_pass)
low_back.defvjp(back_keep, back_low)
EPS = 1e-05
NEG_FILL = -1e+30
HIGH = lax.Precision.HIGHEST

def layer_norm(inputs, ln_gain, ln_shift):
    center = lax.optimization_barrier(jnp.mean(inputs, axis=-1, keepdims=True))
    centered = inputs - center
    spread = lax.optimization_barrier(jnp.mean(centered * centered, axis=-1, keepdims=True))
    return centered * lax.rsqrt(spread + EPS) * ln_gain + ln_shift

def matmul(left_side, right_side):
    return jnp.dot(left_side, right_side, precision=HIGH, preferred_element_type=jnp.float32)

def layer_forward(inputs, length, params):
    w_qkv, bias_q, bias_v, w_out, bias_out, ln1_gain, ln1_bias, w_up, bias_up, w_down, bias_down, ln2_gain, ln2_bias = params
    slot_count = inputs.shape[0]
    normed = low(layer_norm(inputs, ln1_gain, ln1_bias))
    projected = matmul(normed, w_qkv)
    queries = low_back(low(projected[:, :D] + bias_q)).reshape(slot_count, HEADS, HEAD_DIM)
    key_rows = low_back(low(projected[:, D:2 * D])).reshape(slot_count, HEADS, HEAD_DIM)
    value_rows = low_back(low(projected[:, 2 * D:] + bias_v)).reshape(slot_count, HEADS, HEAD_DIM)
    raw_scores = jnp.einsum('qhe,khe->hqk', queries, key_rows, precision=HIGH)
    scores = low_back(raw_scores * HEAD_DIM ** (-0.5))
    positions = jnp.arange(slot_count, dtype=jnp.int32)
    allowed = (positions[None, :] <= positions[:, None]) & (positions[None, :] < length)
    masked = jnp.where(allowed[None], scores, NEG_FILL)
    row_max = lax.optimization_barrier(jnp.max(masked, axis=-1, keepdims=True))
    weights = jnp.where(allowed[None], jnp.exp(masked - row_max), 0.0)
    row_total = lax.optimization_barrier(jnp.sum(weights, axis=-1))
    numerator = low_back(jnp.einsum('hqk,khe->hqe', low(weights), value_rows, precision=HIGH))
    mixed_heads = numerator / row_total[:, :, None]
    mixed_rows = jnp.transpose(mixed_heads, (1, 0, 2)).reshape(slot_count, D)
    attn_out = low_back(matmul(low(mixed_rows), w_out) + bias_out)
    residual = inputs + attn_out
    normed2 = low(layer_norm(residual, ln2_gain, ln2_bias))
    pre_act = low_back(matmul(normed2, w_up) + bias_up)
    activated = low(jax.nn.gelu(pre_act, approximate=False))
    branch = low_back(matmul(activated, w_down) + bias_down)
    return residual + branch

def reference(hidden_in, lengths, cotangent, w_qkv, bias_q, bias_v, w_out, bias_out, ln1_gain, ln1_bias, w_up, bias_up, w_down, bias_down, ln2_gain, ln2_bias):
    params = tuple((weight.astype(jnp.float32) for weight in (w_qkv, bias_q, bias_v, w_out, bias_out, ln1_gain, ln1_bias, w_up, bias_up, w_down, bias_down, ln2_gain, ln2_bias)))
    inputs_all = hidden_in.reshape(-1, SLOTS, D)
    lengths_all = lengths.reshape(-1).astype(jnp.int32)
    cotangent_all = cotangent.reshape(-1, SLOTS, D)
    positions = jnp.arange(SLOTS, dtype=jnp.int32)

    def one_sequence(totals, scan_items):
        inputs, length, upstream = scan_items

        def apply_layer(flat_in, weights_in):
            return layer_forward(flat_in, length, weights_in)
        result, pull_back = jax.vjp(apply_layer, inputs.astype(jnp.float32), params)
        filled = (positions < length).astype(jnp.float32)[:, None]
        d_input, d_params = pull_back(upstream.astype(jnp.float32) * filled)
        totals = jax.tree.map(lambda first_term, second_term: first_term + second_term, totals, d_params)
        return (totals, (result.astype(jnp.bfloat16), d_input))
    zeros_init = tuple((jnp.zeros_like(weight) for weight in params))
    totals, (outputs, d_inputs) = lax.scan(one_sequence, zeros_init, (inputs_all, lengths_all, cotangent_all))
    return (outputs.reshape(hidden_in.shape), d_inputs.reshape(hidden_in.shape), totals[0], totals[1], totals[2], totals[3], totals[4], totals[5], totals[6], totals[7], totals[8], totals[9], totals[10], totals[11], totals[12])
```

```python
import functools

import jax
import jax.numpy as jnp
from jax import lax
from jax.experimental import pallas as pl
from jax.experimental.pallas import tpu as pltpu
from jax.sharding import PartitionSpec as P

HEADS = 16
HEAD_DIM = 64
EPS = 1e-05
NEG_FILL = -1e30
MESH = pl.DeviceIdType.MESH
F32 = jnp.float32
BF16 = jnp.bfloat16
VMEM = pltpu.VMEM
DMA = pltpu.SemaphoreType.DMA
VMEM_LIMIT = 60 * 1024 * 1024
CHUNKS = 12


def layer_norm(inputs, ln_gain, ln_shift):
    center = jnp.mean(inputs, axis=-1, keepdims=True)
    centered = inputs - center
    spread = jnp.mean(centered * centered, axis=-1, keepdims=True)
    return centered * lax.rsqrt(spread + EPS) * ln_gain + ln_shift


def rows_sum(matrix):
    return jnp.sum(matrix.astype(F32), axis=0)


def matmul(left_side, right_side):
    return jnp.dot(left_side, right_side, preferred_element_type=F32)


def dot_nt(a, b):
    return lax.dot_general(a, b, (((1,), (1,)), ((), ())), preferred_element_type=F32)


def dot_tn(a, b):
    return lax.dot_general(a, b, (((0,), (0,)), ((), ())), preferred_element_type=F32)


def place():
    d = lax.axis_index("ctx")
    z = lax.axis_index("fsdp")
    return d, d // 4, lax.rem(d // 2, 2), lax.rem(d, 2), z


def remote(src, dst, send, recv, device):
    return pltpu.make_async_remote_copy(
        src_ref=src, dst_ref=dst, send_sem=send, recv_sem=recv, device_id=device, device_id_type=MESH
    )


def greet(devices):
    barrier = pltpu.get_barrier_semaphore()
    for device in devices:
        pl.semaphore_signal(barrier, inc=1, device_id=device, device_id_type=MESH)
    pl.semaphore_wait(barrier, len(devices))


def run_stages(stages, offsets, count):
    @pl.loop(0, count + offsets[-1])
    def _(step):
        for index in reversed(range(len(stages))):
            chunk = step - offsets[index]

            @pl.when((chunk >= 0) & (chunk < count))
            def _():
                stages[index](chunk)


def gather_kernel(count, offsets, src, small, out, small_out, local_sem, vs, vr, zs, zr, xs, xr, cs, cr):
    d, y, x, c, z = place()
    x_nb, y_nb, c_nb = (d + 2 - 4 * x, z), (d + 4 - 8 * y, z), (d + 1 - 2 * c, z)
    line = [(d, lax.rem(z + k, 4)) for k in (1, 2, 3)]
    greet([x_nb, y_nb, c_nb] + line)
    local = pltpu.make_async_copy(src, out.at[:, z], local_sem)
    local.start()

    def small_copy(k):
        return remote(small, small_out.at[z], vs.at[k], vr.at[k], line[k])

    def small_recv(k):
        return remote(small, small_out.at[lax.rem(z + 3 - k, 4)], vs.at[k], vr.at[k], line[k])

    for k in range(3):
        small_copy(k).start()
    small_out[z] = small[...]

    def z_copy(chunk, k, down):
        piece = z + k if down else z - k
        ref = src.at[chunk, y, x, c] if k == 0 else out.at[chunk, piece, y, x, c]
        target = (d, z - 1) if down else (d, z + 1)
        return remote(ref, out.at[chunk, piece, y, x, c], zs.at[chunk, down, k], zr.at[chunk, down, k], target)

    def z_recv(chunk, k, down):
        piece = z + 1 + k if down else z - 1 - k
        ref = out.at[chunk, piece, y, x, c]
        return remote(ref, ref, zs.at[chunk, down, k], zr.at[chunk, down, k], x_nb)

    def z_start(chunk, k):
        @pl.when((z < 3) & (z >= k))
        def _():
            z_copy(chunk, k, 0).start()

        @pl.when((z > 0) & (z + k <= 3))
        def _():
            z_copy(chunk, k, 1).start()

    def z_wait(chunk, k):
        @pl.when(z >= k + 1)
        def _():
            z_recv(chunk, k, 0).wait_recv()

        @pl.when(z + k + 1 <= 3)
        def _():
            z_recv(chunk, k, 1).wait_recv()

    def first(chunk, i, axis):
        ref = out.at[chunk, lax.rem(z + 1 + i, 4), y, x, c, axis]
        return remote(ref, ref, xs.at[chunk, 0, axis, i], xr.at[chunk, 0, axis, i], y_nb if axis else x_nb)

    def first_recv(chunk, i, axis):
        piece = lax.rem(z + 1 + i, 4)
        ref = out.at[chunk, piece, 1 - y, x, c, 1] if axis else out.at[chunk, piece, y, 1 - x, c, 0]
        return remote(ref, ref, xs.at[chunk, 0, axis, i], xr.at[chunk, 0, axis, i], y_nb if axis else x_nb)

    def second(chunk, i, axis):
        piece = lax.rem(z + 1 + i, 4)
        ref = out.at[chunk, piece, :, x, c, 1] if axis else out.at[chunk, piece, y, :, c, 0]
        return remote(ref, ref, xs.at[chunk, 1, axis, i], xr.at[chunk, 1, axis, i], x_nb if axis else y_nb)

    def second_recv(chunk, i, axis):
        piece = lax.rem(z + 1 + i, 4)
        ref = out.at[chunk, piece, :, 1 - x, c, 1] if axis else out.at[chunk, piece, 1 - y, :, c, 0]
        return remote(ref, ref, xs.at[chunk, 1, axis, i], xr.at[chunk, 1, axis, i], x_nb if axis else y_nb)

    def across(chunk, i, core):
        ref = out.at[chunk, lax.rem(z + 1 + i, 4), :, :, core]
        return remote(ref, ref, cs.at[chunk, i], cr.at[chunk, i], c_nb)

    def stage0(chunk):
        z_start(chunk, 0)

    def stage1(chunk):
        z_wait(chunk, 0)
        z_start(chunk, 1)

    def stage2(chunk):
        z_wait(chunk, 1)
        z_start(chunk, 2)

    def stage3(chunk):
        z_wait(chunk, 2)
        for i in range(3):
            for axis in range(2):
                first(chunk, i, axis).start()

    def stage4(chunk):
        for i in range(3):
            for axis in range(2):
                first_recv(chunk, i, axis).wait_recv()
        for i in range(3):
            for axis in range(2):
                second(chunk, i, axis).start()

    def stage5(chunk):
        for i in range(3):
            for axis in range(2):
                second_recv(chunk, i, axis).wait_recv()
        for i in range(3):
            across(chunk, i, c).start()

    def stage6(chunk):
        for i in range(3):
            across(chunk, i, 1 - c).wait_recv()
        for i in range(3):
            across(chunk, i, c).wait_send()
            for axis in range(2):
                first(chunk, i, axis).wait_send()
                second(chunk, i, axis).wait_send()
        for k in range(3):
            @pl.when((z < 3) & (z >= k))
            def _():
                z_copy(chunk, k, 0).wait_send()

            @pl.when((z > 0) & (z + k <= 3))
            def _():
                z_copy(chunk, k, 1).wait_send()

    run_stages([stage0, stage1, stage2, stage3, stage4, stage5, stage6], offsets, count)
    for k in range(3):
        small_recv(k).wait_recv()
        small_copy(k).wait_send()
    local.wait()


def gather_weights(packed, small):
    count, rows, width = packed.shape
    vm, anywhere = pl.BlockSpec(memory_space=VMEM), pl.BlockSpec(memory_space=pl.ANY)
    out, small_out = pl.pallas_call(
        functools.partial(gather_kernel, count, (0, 1, 2, 3, 5, 7, 8)),
        out_shape=(
            jax.ShapeDtypeStruct((count, 4, 2, 2, 2, 2, rows // 16, width), BF16),
            jax.ShapeDtypeStruct((4,) + small.shape, BF16),
        ),
        in_specs=[vm, vm],
        out_specs=(anywhere, vm),
        scratch_shapes=[
            DMA, DMA((3,)), DMA((3,)),
            DMA((count, 2, 3)), DMA((count, 2, 3)),
            DMA((count, 2, 2, 3)), DMA((count, 2, 2, 3)),
            DMA((count, 3)), DMA((count, 3)),
        ],
        compiler_params=pltpu.CompilerParams(
            collective_id=0, has_side_effects=True, vmem_limit_bytes=24 * 1024 * 1024
        ),
        name="gather_weights",
    )(packed.reshape(count, 2, 2, 2, 2, rows // 16, width), small)
    return out.reshape(count, 4 * rows, width), small_out


def reduce_kernel(
    bounds, offsets, *refs
):
    count = bounds[-1]
    parts, small = refs[: len(bounds) - 1], refs[len(bounds) - 1]
    out, small_out = refs[len(bounds)], refs[len(bounds) + 1]
    (acc, core_in, x_in, y_in, x_in2, y_in2, up_in, down_in, small_in,
     ls, cs, cr, s1, r1, s2, r2, zs, zr, s3, r3, s4, r4, s5, r5, vs, vr) = refs[len(bounds) + 2 :]
    d, y, x, c, z = place()
    x_nb, y_nb, c_nb = (d + 2 - 4 * x, z), (d + 4 - 8 * y, z), (d + 1 - 2 * c, z)
    line = [(d, lax.rem(z + k, 4)) for k in (1, 2, 3)]
    greet([x_nb, y_nb, c_nb] + line)

    def load(ref, chunk, slot):
        return pltpu.make_async_copy(ref.at[chunk, :, :, :, c], acc.at[slot], ls.at[slot])

    def core_send(ref, chunk, slot):
        return remote(ref.at[chunk, :, :, :, 1 - c], core_in.at[slot], cs.at[slot], cr.at[slot], c_nb)

    def x1(k):
        return remote(acc.at[k, :, :, 1 - x, 0], x_in.at[k], s1.at[k, 0], r1.at[k, 0], x_nb)

    def y1(k):
        return remote(acc.at[k, :, 1 - y, :, 1], y_in.at[k], s1.at[k, 1], r1.at[k, 1], y_nb)

    def y2(k):
        return remote(acc.at[k, :, 1 - y, x, 0], y_in2.at[k], s2.at[k, 0], r2.at[k, 0], y_nb)

    def x2(k):
        return remote(acc.at[k, :, y, 1 - x, 1], x_in2.at[k], s2.at[k, 1], r2.at[k, 1], x_nb)

    def up(k, i):
        return remote(acc.at[k, z + 3 - i, y, x], up_in.at[k, i], zs.at[k, 0, i], zr.at[k, 0, i], (d, z + 1))

    def down(k, i):
        return remote(acc.at[k, z - 3 + i, y, x], down_in.at[k, i], zs.at[k, 1, i], zr.at[k, 1, i], (d, z - 1))

    def up_wait(k, i):
        remote(up_in.at[k, i], up_in.at[k, i], zs.at[k, 0, i], zr.at[k, 0, i], c_nb).wait_recv()

    def down_wait(k, i):
        remote(down_in.at[k, i], down_in.at[k, i], zs.at[k, 1, i], zr.at[k, 1, i], c_nb).wait_recv()

    def g1(k, axis):
        ref = out.at[k, y, x, c, axis]
        return remote(ref, ref, s3.at[k, axis], r3.at[k, axis], y_nb if axis else x_nb)

    def g1_recv(k, axis):
        ref = out.at[k, 1 - y, x, c, 1] if axis else out.at[k, y, 1 - x, c, 0]
        return remote(ref, ref, s3.at[k, axis], r3.at[k, axis], y_nb if axis else x_nb)

    def g2(k, axis):
        ref = out.at[k, :, x, c, 1] if axis else out.at[k, y, :, c, 0]
        return remote(ref, ref, s4.at[k, axis], r4.at[k, axis], x_nb if axis else y_nb)

    def g2_recv(k, axis):
        ref = out.at[k, :, 1 - x, c, 1] if axis else out.at[k, 1 - y, :, c, 0]
        return remote(ref, ref, s4.at[k, axis], r4.at[k, axis], x_nb if axis else y_nb)

    def g3(k, core):
        ref = out.at[k, :, :, core]
        return remote(ref, ref, s5.at[k], r5.at[k], c_nb)

    def z_send(k, i):
        @pl.when((z < 3) & (z <= i))
        def _():
            up(k, i).start()

        @pl.when((z > 0) & (z >= 3 - i))
        def _():
            down(k, i).start()

    def z_add(k, i):
        @pl.when((z >= 1) & (z - 1 <= i))
        def _():
            up_wait(k, i)
            acc[k, z + 2 - i, y, x] += up_in[k, i]

        @pl.when((z <= 2) & (z + 1 >= 3 - i))
        def _():
            down_wait(k, i)
            acc[k, z - 2 + i, y, x] += down_in[k, i]

    def stage0(k):
        for index, part in enumerate(parts):
            low, high = bounds[index], bounds[index + 1]

            @pl.when((k >= low) & (k < high))
            def _():
                core_send(part, k - low, k).start()
                load(part, k - low, k).start()

    def stage1(k):
        load(parts[0], 0, k).wait()
        core_send(parts[0], 0, k).wait_recv()
        for piece in range(4):
            acc[k, piece] += core_in[k, piece]
        x1(k).start()
        y1(k).start()

    def stage2(k):
        x1(k).wait_recv()
        y1(k).wait_recv()
        acc[k, :, :, x, 0] += x_in[k]
        acc[k, :, y, :, 1] += y_in[k]
        y2(k).start()
        x2(k).start()

    def stage3(k):
        y2(k).wait_recv()
        x2(k).wait_recv()
        acc[k, :, y, x, 0] += y_in2[k]
        acc[k, :, y, x, 1] += x_in2[k]
        z_send(k, 0)

    def stage4(k):
        z_add(k, 0)
        z_send(k, 1)

    def stage5(k):
        z_add(k, 1)
        z_send(k, 2)

    def stage6(k):
        z_add(k, 2)
        out[k, y, x, c] = acc[k, z, y, x]
        g1(k, 0).start()
        g1(k, 1).start()

    def stage7(k):
        for axis in range(2):
            g1_recv(k, axis).wait_recv()
        for axis in range(2):
            g2(k, axis).start()

    def stage8(k):
        for axis in range(2):
            g2_recv(k, axis).wait_recv()
        g3(k, c).start()

    def stage9(k):
        g3(k, 1 - c).wait_recv()
        g3(k, c).wait_send()
        core_send(parts[0], 0, k).wait_send()
        x1(k).wait_send()
        y1(k).wait_send()
        x2(k).wait_send()
        y2(k).wait_send()
        for axis in range(2):
            g1(k, axis).wait_send()
            g2(k, axis).wait_send()
        for i in range(3):
            @pl.when((z < 3) & (z <= i))
            def _():
                up(k, i).wait_send()

            @pl.when((z > 0) & (z >= 3 - i))
            def _():
                down(k, i).wait_send()

    for step, nb in enumerate((c_nb, x_nb, y_nb)):
        if step == 0:
            small_out[0] = small[...]
        copy = remote(small_out.at[step], small_in.at[step], vs.at[step], vr.at[step], nb)
        copy.start()
        copy.wait()
        small_out[step + 1] = small_out[step] + small_in[step]
    copies = [remote(small_out.at[3], small_in.at[3 + k], vs.at[3 + k], vr.at[3 + k], line[k]) for k in range(3)]
    for copy in copies:
        copy.start()

    run_stages(
        [stage0, stage1, stage2, stage3, stage4, stage5, stage6, stage7, stage8, stage9], offsets, count
    )
    for copy in copies:
        copy.wait()
    small_out[4] = small_out[3] + small_in[3] + small_in[4] + small_in[5]


def reduce_gradients(parts, small, collective):
    rows, width = parts[0].shape[1] // 4, parts[0].shape[2]
    piece = rows // 16
    bounds = [0]
    for part in parts:
        bounds.append(bounds[-1] + part.shape[0])
    n = bounds[-1]
    vm, anywhere = pl.BlockSpec(memory_space=VMEM), pl.BlockSpec(memory_space=pl.ANY)
    out, small_out = pl.pallas_call(
        functools.partial(reduce_kernel, tuple(bounds), (0, 1, 3, 5, 6, 7, 8, 9, 10, 11)),
        out_shape=(
            jax.ShapeDtypeStruct((n, 2, 2, 2, 2, piece, width), BF16),
            jax.ShapeDtypeStruct((5,) + small.shape, F32),
        ),
        in_specs=[anywhere] * len(parts) + [vm],
        out_specs=(vm, vm),
        scratch_shapes=[
            VMEM((n, 4, 2, 2, 2, piece, width), BF16),
            VMEM((n, 4, 2, 2, 2, piece, width), BF16),
            VMEM((n, 4, 2, piece, width), BF16),
            VMEM((n, 4, 2, piece, width), BF16),
            VMEM((n, 4, piece, width), BF16),
            VMEM((n, 4, piece, width), BF16),
            VMEM((n, 3, 2, piece, width), BF16),
            VMEM((n, 3, 2, piece, width), BF16),
            VMEM((6,) + small.shape, F32),
            DMA((n,)), DMA((n,)), DMA((n,)),
            DMA((n, 2)), DMA((n, 2)), DMA((n, 2)), DMA((n, 2)),
            DMA((n, 2, 3)), DMA((n, 2, 3)),
            DMA((n, 2)), DMA((n, 2)), DMA((n, 2)), DMA((n, 2)),
            DMA((n,)), DMA((n,)), DMA((6,)), DMA((6,)),
        ],
        compiler_params=pltpu.CompilerParams(
            collective_id=collective, has_side_effects=True, vmem_limit_bytes=VMEM_LIMIT
        ),
        name="reduce_gradients",
    )(*[p.reshape(p.shape[0], 4, 2, 2, 2, 2, piece, width) for p in parts], small)
    return out.reshape(n, rows, width), small_out[4]


def head_lanes(width):
    return lax.broadcasted_iota(jnp.int32, (1, width), 1) // HEAD_DIM


def attend(q, k, v, length, block, put):
    slots = k.shape[0]
    key_pos = lax.broadcasted_iota(jnp.int32, (1, slots), 1)
    bias = jnp.where(key_pos < length, 0.0, NEG_FILL).astype(F32)
    width = k.shape[1]
    lanes = head_lanes(width)
    causal = lax.broadcasted_iota(jnp.int32, (block, block), 1) <= lax.broadcasted_iota(
        jnp.int32, (block, block), 0
    )
    for start in range(0, slots, block):
        stop = start + block
        q_block = q[start:stop, :]
        sums, levels = None, None
        for head in range(width // HEAD_DIM):
            q_head = jnp.where(lanes == head, q_block, jnp.zeros_like(q_block)) * jnp.asarray(HEAD_DIM**-0.5, BF16)
            scores = dot_nt(q_head, k[:stop, :]) + bias[:, :stop]
            last = jnp.where(causal, scores[:, start:], NEG_FILL)
            top = jnp.max(last, axis=1, keepdims=True)
            if start:
                top = jnp.maximum(top, jnp.max(scores[:, :start], axis=1, keepdims=True))
                scores = jnp.concatenate([scores[:, :start], last], axis=1)
            else:
                scores = last
            weights = jnp.exp(scores - top)
            total = jnp.sum(weights, axis=1, keepdims=True)
            mixed = matmul(weights.astype(BF16), v[:stop, :]) / total
            level = top + jnp.log(total)
            sums = mixed if sums is None else jnp.where(lanes == head, mixed, sums)
            level = jnp.broadcast_to(level, mixed.shape)
            levels = level if levels is None else jnp.where(lanes == head, level, levels)
        put(start, stop, sums, levels)


def peers():
    d, z = lax.axis_index("ctx"), lax.axis_index("fsdp")
    to = [lax.rem(d + k, 8) for k in range(1, 8)]
    come = [lax.rem(d + 8 - k, 8) for k in range(1, 8)]
    return d, z, to, come


def lanes_of(index):
    return pl.ds(pl.multiple_of(index * 128, 128), 128)


def rows_of(index):
    return pl.ds(pl.multiple_of(index * 128, 128), 128)


def attention_forward_kernel(qkv, lengths, low_out, buf, o_out, level_out, mine, ls, s1, r1, lt, s2, r2):
    d, z, to, come = peers()
    greet([(p, z) for p in to])
    seqs = qkv.shape[1]

    def send(s, k):
        return remote(
            qkv.at[:, s, :, lanes_of(to[k])], buf.at[s, :, rows_of(d), :], s1.at[s, k], r1.at[s, k], (to[k], z)
        )

    def recv(s, k):
        ref = buf.at[s, :, rows_of(come[k]), :]
        return remote(ref, ref, s1.at[s, k], r1.at[s, k], (to[k], z))

    def keep(s):
        return pltpu.make_async_copy(qkv.at[:, s, :, lanes_of(d)], buf.at[s, :, rows_of(d), :], ls.at[s])

    def send_back(s, k):
        return remote(
            mine.at[s, rows_of(to[k]), :], low_out.at[s, :, lanes_of(d)], s2.at[s, k], r2.at[s, k], (to[k], z)
        )

    def recv_back(s, k):
        ref = low_out.at[s, :, lanes_of(come[k])]
        return remote(ref, ref, s2.at[s, k], r2.at[s, k], (to[k], z))

    def keep_back(s):
        return pltpu.make_async_copy(mine.at[s, rows_of(d), :], low_out.at[s, :, lanes_of(d)], lt.at[s])

    @pl.loop(0, seqs)
    def _(s):
        for k in range(7):
            send(s, k).start()
        keep(s).start()

    @pl.loop(0, seqs)
    def _(s):
        keep(s).wait()
        for k in range(7):
            recv(s, k).wait_recv()

        def put(start, stop, mixed, level):
            o_out[s, start:stop, :] = mixed
            level_out[s, start:stop, :] = level
            mine[s, start:stop, :] = mixed.astype(BF16)

        attend(buf.at[s, 0], buf.at[s, 1], buf.at[s, 2], lengths[s], 256, put)
        for k in range(7):
            send_back(s, k).start()
        keep_back(s).start()

    @pl.loop(0, seqs)
    def _(s):
        keep_back(s).wait()
        for k in range(7):
            recv_back(s, k).wait_recv()
            send(s, k).wait_send()
            send_back(s, k).wait_send()


def attention_forward(qkv, lengths):
    _, seqs, slots, width = qkv.shape
    vm = pl.BlockSpec(memory_space=VMEM)
    return pl.pallas_call(
        attention_forward_kernel,
        out_shape=(
            jax.ShapeDtypeStruct((seqs, slots, width), BF16),
            jax.ShapeDtypeStruct((seqs, 3, slots * 8, 128), BF16),
            jax.ShapeDtypeStruct((seqs, slots * 8, 128), F32),
            jax.ShapeDtypeStruct((seqs, slots * 8, 128), F32),
        ),
        in_specs=[vm, pl.BlockSpec(memory_space=pltpu.SMEM)],
        out_specs=(vm, vm, vm, vm),
        scratch_shapes=[
            VMEM((seqs, slots * 8, 128), BF16),
            DMA((seqs,)), DMA((seqs, 7)), DMA((seqs, 7)),
            DMA((seqs,)), DMA((seqs, 7)), DMA((seqs, 7)),
        ],
        compiler_params=pltpu.CompilerParams(
            collective_id=1, has_side_effects=True, vmem_limit_bytes=VMEM_LIMIT
        ),
        name="attention_forward",
    )(qkv, lengths)


def attend_back(q, k, v, o, levels, dm, length, block, put_query, put_key):
    slots, width = k.shape
    key_pos = lax.broadcasted_iota(jnp.int32, (1, slots), 1)
    bias = jnp.where(key_pos < length, 0.0, NEG_FILL).astype(F32)
    lanes = head_lanes(width)
    causal = lax.broadcasted_iota(jnp.int32, (block, block), 1) <= lax.broadcasted_iota(
        jnp.int32, (block, block), 0
    )
    scale = jnp.asarray(HEAD_DIM**-0.5, BF16)
    for start in range(0, slots, block):
        stop = start + block
        q_block = q[start:stop, :] * scale
        d_block = dm[start:stop, :]
        product = d_block.astype(F32) * o[start:stop, :]
        q_turned, d_turned = q_block.T, d_block.T
        d_query, d_keys, d_values = None, [], []
        for head in range(width // HEAD_DIM):
            here = lanes == head
            q_head = jnp.where(here, q_block, jnp.zeros_like(q_block))
            d_head = jnp.where(here, d_block, jnp.zeros_like(d_block))
            total = jnp.sum(jnp.where(here, product, 0.0), axis=1, keepdims=True)
            level = levels[start:stop, head * HEAD_DIM : head * HEAD_DIM + 1]
            scores = dot_nt(q_head, k[:stop, :]) + bias[:, :stop]
            last = jnp.where(causal, scores[:, start:], NEG_FILL)
            scores = jnp.concatenate([scores[:, :start], last], axis=1) if start else last
            weights = jnp.exp(scores - level)
            d_weight = dot_nt(d_head, v[:stop, :]) - total
            d_score = (weights * d_weight).astype(BF16)
            part = matmul(d_score, k[:stop, :])
            d_query = part if d_query is None else jnp.where(here, part, d_query)
            cut = slice(head * HEAD_DIM, (head + 1) * HEAD_DIM)
            d_values.append(matmul(d_turned[cut, :], weights.astype(BF16)))
            d_keys.append(matmul(q_turned[cut, :], d_score))
        put_query(start, stop, d_query * (HEAD_DIM**-0.5))
        put_key(start, stop, jnp.concatenate(d_keys, axis=0), jnp.concatenate(d_values, axis=0))


def attention_backward_kernel(
    dm_home, buf, o, levels, lengths, out, dm, mine, turned, ls, s1, r1, lt, s2, r2
):
    d, z, to, come = peers()
    greet([(p, z) for p in to])
    seqs = dm_home.shape[0]

    def send(s, k):
        return remote(
            dm_home.at[s, :, lanes_of(to[k])], dm.at[s, rows_of(d), :], s1.at[s, k], r1.at[s, k], (to[k], z)
        )

    def recv(s, k):
        ref = dm.at[s, rows_of(come[k]), :]
        return remote(ref, ref, s1.at[s, k], r1.at[s, k], (to[k], z))

    def keep(s):
        return pltpu.make_async_copy(dm_home.at[s, :, lanes_of(d)], dm.at[s, rows_of(d), :], ls.at[s])

    def send_back(s, k):
        return remote(
            mine.at[s, :, rows_of(to[k]), :], out.at[:, s, :, lanes_of(d)], s2.at[s, k], r2.at[s, k], (to[k], z)
        )

    def recv_back(s, k):
        ref = out.at[:, s, :, lanes_of(come[k])]
        return remote(ref, ref, s2.at[s, k], r2.at[s, k], (to[k], z))

    def keep_back(s):
        return pltpu.make_async_copy(mine.at[s, :, rows_of(d), :], out.at[:, s, :, lanes_of(d)], lt.at[s])

    @pl.loop(0, seqs)
    def _(s):
        for k in range(7):
            send(s, k).start()
        keep(s).start()

    @pl.loop(0, seqs)
    def _(s):
        keep(s).wait()
        for k in range(7):
            recv(s, k).wait_recv()
        turned[...] = jnp.zeros_like(turned)

        def put_query(start, stop, value):
            mine[s, 0, start:stop, :] = value.astype(BF16)

        def put_key(start, stop, d_key, d_value):
            turned[0, :, :stop] += d_key
            turned[1, :, :stop] += d_value

        attend_back(
            buf.at[s, 0], buf.at[s, 1], buf.at[s, 2], o.at[s], levels.at[s], dm.at[s], lengths[s], 256,
            put_query, put_key,
        )
        mine[s, 1] = turned[0].T.astype(BF16)
        mine[s, 2] = turned[1].T.astype(BF16)
        for k in range(7):
            send_back(s, k).start()
        keep_back(s).start()

    @pl.loop(0, seqs)
    def _(s):
        keep_back(s).wait()
        for k in range(7):
            recv_back(s, k).wait_recv()
            send(s, k).wait_send()
            send_back(s, k).wait_send()


def attention_backward(dm_home, buf, o, levels, lengths):
    seqs, slots, width = dm_home.shape
    vm = pl.BlockSpec(memory_space=VMEM)
    return pl.pallas_call(
        attention_backward_kernel,
        out_shape=jax.ShapeDtypeStruct((3, seqs, slots, width), BF16),
        in_specs=[vm, vm, vm, vm, pl.BlockSpec(memory_space=pltpu.SMEM)],
        out_specs=vm,
        scratch_shapes=[
            VMEM((seqs, slots * 8, 128), BF16),
            VMEM((seqs, 3, slots * 8, 128), BF16),
            VMEM((2, 128, slots * 8), F32),
            DMA((seqs,)), DMA((seqs, 7)), DMA((seqs, 7)),
            DMA((seqs,)), DMA((seqs, 7)), DMA((seqs, 7)),
        ],
        compiler_params=pltpu.CompilerParams(
            collective_id=2, has_side_effects=True, vmem_limit_bytes=VMEM_LIMIT
        ),
        name="attention_backward",
    )(dm_home, buf, o, levels, lengths)


def feed_kernel(x, d_out, w_up, w_down, bias, y, dx, g_up, g_down, g_bias, x_turned, act, d_pre):
    tile = 256
    hidden = w_up.shape[2]

    @pl.when(pl.program_id(0) == 0)
    def _():
        y[...] = jnp.zeros_like(y)
        dx[...] = jnp.zeros_like(dx)
        x_turned[...] = x[...].T

    @pl.loop(0, hidden // tile)
    def _(n):
        cut = pl.ds(pl.multiple_of(n * tile, tile), tile)
        pre = matmul(x[...], w_up[0, :, cut]) + bias[0, :, cut].astype(F32)
        cumulative = 0.5 + 0.5 * lax.erf(pre * (0.5**0.5))
        active = (pre * cumulative).astype(BF16)
        act[:, cut] = active
        slope = cumulative + pre * (jnp.exp(-0.5 * pre * pre) * 0.3989422804014327)
        back = dot_nt(d_out[...], w_down[0, cut, :]) * slope
        low = back.astype(BF16)
        d_pre[:, cut] = low
        g_bias[0, :, cut] = jnp.sum(low.astype(F32), axis=0, keepdims=True)
        g_down[0, cut, :] = matmul(active.T, d_out[...]).astype(BF16)
        g_up[0, :, cut] = matmul(x_turned[...], low).astype(BF16)

    @pl.loop(0, y.shape[1] // tile)
    def _(n):
        cut = pl.ds(pl.multiple_of(n * tile, tile), tile)
        y[:, cut] += matmul(act[...], w_down[0, :, cut])
        dx[:, cut] += dot_nt(d_pre[...], w_up[0, cut, :])


def feed_forward(x, d_out, weights, bias, first_up, first_down, blocks):
    rows, width = x.shape
    hidden = weights.shape[2]
    whole = pl.BlockSpec((rows, width), lambda j: (0, 0))
    return pl.pallas_call(
        feed_kernel,
        grid=(blocks,),
        out_shape=(
            jax.ShapeDtypeStruct((rows, width), F32),
            jax.ShapeDtypeStruct((rows, width), F32),
            jax.ShapeDtypeStruct((blocks, width, hidden), BF16),
            jax.ShapeDtypeStruct((blocks, hidden, width), BF16),
            jax.ShapeDtypeStruct((blocks, 1, hidden), F32),
        ),
        in_specs=[
            whole,
            whole,
            pl.BlockSpec((1, width, hidden), lambda j: (first_up + j, 0, 0)),
            pl.BlockSpec((1, hidden, width), lambda j: (first_down + j, 0, 0)),
            pl.BlockSpec((1, 1, hidden), lambda j: (j, 0, 0)),
        ],
        out_specs=(
            whole,
            whole,
            pl.BlockSpec((1, width, hidden), lambda j: (j, 0, 0)),
            pl.BlockSpec((1, hidden, width), lambda j: (j, 0, 0)),
            pl.BlockSpec((1, 1, hidden), lambda j: (j, 0, 0)),
        ),
        scratch_shapes=[VMEM((width, rows), BF16), VMEM((rows, hidden), BF16), VMEM((rows, hidden), BF16)],
        compiler_params=pltpu.CompilerParams(
            dimension_semantics=("arbitrary",), vmem_limit_bytes=VMEM_LIMIT
        ),
        cost_estimate=pl.CostEstimate(
            flops=12 * blocks * rows * width * hidden,
            bytes_accessed=8 * blocks * width * hidden + 12 * rows * width,
            transcendentals=2 * blocks * rows * hidden,
        ),
        name="feed_forward",
    )(x, d_out, weights, weights, bias)


def any_gather(packed, small):
    return (
        lax.all_gather(packed, "fsdp", axis=1, tiled=True),
        lax.all_gather(small, "fsdp", axis=0, tiled=False),
    )


def any_reduce(parts, small):
    out = []
    for part in parts:
        mine = lax.psum_scatter(part, "fsdp", scatter_dimension=1, tiled=True)
        out.append(lax.psum(mine, "ctx"))
    return jnp.concatenate(out, axis=0), lax.psum(small, ("ctx", "fsdp"))


def any_forward(qkv, lengths):
    wide = lax.all_to_all(qkv, "ctx", split_axis=3, concat_axis=2, tiled=True)
    wide = jnp.swapaxes(wide, 0, 1)

    def one(item):
        rows, length = item
        mixed, levels = [], []

        def put(start, stop, part, level):
            mixed.append(part)
            levels.append(level)

        attend(rows[0], rows[1], rows[2], length, rows.shape[1], put)
        return mixed[0], levels[0]

    mixed, levels = lax.map(one, (wide, lengths))
    low = lax.all_to_all(mixed.astype(BF16), "ctx", split_axis=1, concat_axis=2, tiled=True)
    return low, wide, mixed, levels


def any_backward(dm_home, wide, mixed, levels, lengths):
    dm = lax.all_to_all(dm_home, "ctx", split_axis=2, concat_axis=1, tiled=True)

    def one(item):
        rows, part, level, upstream, length = item
        found = {}

        def put_query(start, stop, value):
            found[0] = value.astype(BF16)

        def put_key(start, stop, d_key, d_value):
            found[1], found[2] = d_key.T.astype(BF16), d_value.T.astype(BF16)

        attend_back(
            rows[0], rows[1], rows[2], part, level, upstream, length, rows.shape[1], put_query, put_key
        )
        return jnp.stack([found[0], found[1], found[2]])

    out = lax.map(one, (wide, mixed, levels, dm, lengths))
    out = lax.all_to_all(out, "ctx", split_axis=2, concat_axis=3, tiled=True)
    return jnp.swapaxes(out, 0, 1)


def body(
    routed,
    hidden_in,
    lengths,
    cotangent,
    w_qkv,
    bias_q,
    bias_v,
    w_out,
    bias_out,
    ln1_gain,
    ln1_bias,
    w_up,
    bias_up,
    w_down,
    bias_down,
    ln2_gain,
    ln2_bias,
):
    batch, seqs, slots, width = hidden_in.shape
    count = batch * seqs
    rows = count * slots
    shard = w_qkv.shape[0]
    shards = width // shard
    blocks = w_up.shape[1] // width

    up_parts = jnp.transpose(w_up.reshape(shard, shards, blocks, shard), (2, 0, 1, 3)).reshape(blocks, shard, width)
    packed = jnp.concatenate(
        [
            jnp.transpose(w_qkv.reshape(shard, 3, width), (1, 0, 2)),
            w_out[None],
            up_parts,
            w_down.reshape(blocks, shard, width),
        ],
        axis=0,
    )
    vectors = [bias_q, bias_v, bias_out, ln1_gain, ln1_bias, bias_down, ln2_gain, ln2_bias]
    small = jnp.concatenate([jnp.stack(vectors), bias_up.reshape(blocks, shard)], axis=0)
    small = jnp.pad(small, ((0, 16 - small.shape[0]), (0, 0)))
    weights, small_all = (gather_weights if routed else any_gather)(packed, small)
    small_all = jnp.transpose(small_all, (1, 0, 2)).reshape(16, width)
    full = small_all.astype(F32)
    full_q, full_v, full_bias_out, gain_one, shift_one, full_bias_down, gain_two, shift_two = [
        full[i] for i in range(8)
    ]
    full_up = small_all[8 : 8 + blocks].reshape(blocks, 1, width)

    flat_in = hidden_in.reshape(rows, width).astype(F32)
    normed = layer_norm(flat_in, gain_one, shift_one).astype(BF16)
    queries = (matmul(normed, weights[0]) + full_q).astype(BF16)
    key_rows = matmul(normed, weights[1]).astype(BF16)
    value_rows = (matmul(normed, weights[2]) + full_v).astype(BF16)
    qkv = jnp.stack([queries, key_rows, value_rows]).reshape(3, count, slots, width)
    flat_lengths = lengths.reshape(count)
    mixed_home, wide, mixed, levels = (attention_forward if routed else any_forward)(qkv, flat_lengths)
    mixed_low = mixed_home.reshape(rows, width)
    residual = flat_in + matmul(mixed_low, weights[3]) + full_bias_out
    normed2 = layer_norm(residual, gain_two, shift_two).astype(BF16)

    position = lax.axis_index("ctx") * slots + jnp.arange(slots, dtype=jnp.int32)
    filled = (position[None, :] < flat_lengths[:, None]).astype(F32).reshape(rows, 1)
    d_out = cotangent.reshape(rows, width).astype(F32) * filled
    d_branch = d_out.astype(BF16)
    fed, d_normed2, grad_up, grad_down, grad_bias_up = feed_forward(
        normed2, d_branch, weights, full_up, 4, 4 + blocks, blocks
    )
    output = (residual + fed + full_bias_down).astype(BF16)
    norm_pull_two = jax.vjp(layer_norm, residual, gain_two, shift_two)[1]
    d_resid_norm, grad_ln2_gain, grad_ln2_bias = norm_pull_two(d_normed2)
    d_residual = d_out + d_resid_norm
    d_attn = d_residual.astype(BF16)
    grad_out = dot_tn(mixed_low, d_attn).astype(BF16)
    d_mixed = dot_nt(d_attn, weights[3]).astype(BF16).reshape(count, slots, width)
    d_qkv = (attention_backward if routed else any_backward)(d_mixed, wide, mixed, levels, flat_lengths)
    d_qkv = d_qkv.reshape(3, rows, width)
    grad_qkv = jnp.stack([dot_tn(normed, d_qkv[i]).astype(BF16) for i in range(3)])
    d_normed = sum(dot_nt(d_qkv[i], weights[i]) for i in range(3))
    norm_pull_one = jax.vjp(layer_norm, flat_in, gain_one, shift_one)[1]
    d_input_norm, grad_ln1_gain, grad_ln1_bias = norm_pull_one(d_normed)
    grad_hidden = d_residual + d_input_norm

    small_grads = jnp.stack(
        [
            rows_sum(d_qkv[0]),
            rows_sum(d_qkv[2]),
            rows_sum(d_attn),
            grad_ln1_gain,
            grad_ln1_bias,
            jnp.sum(d_out, axis=0),
            grad_ln2_gain,
            grad_ln2_bias,
        ]
        + [grad_bias_up[j, 0] for j in range(blocks)]
        + [jnp.zeros((width,), F32)] * (8 - blocks)
    )
    parts = [grad_qkv, grad_out[None], grad_up, grad_down]
    if routed:
        sums, small_sums = reduce_gradients(parts, small_grads, 3)
    else:
        sums, small_sums = any_reduce(parts, small_grads)
    mine = lax.dynamic_slice_in_dim(small_sums, lax.axis_index("fsdp") * shard, shard, 1)
    sums = sums.astype(F32)
    out_qkv = jnp.transpose(sums[:3], (1, 0, 2)).reshape(shard, 3 * width)
    out_up = jnp.transpose(sums[4 : 4 + blocks].reshape(blocks, shard, shards, shard), (1, 2, 0, 3))
    return (
        output.reshape(hidden_in.shape),
        grad_hidden.reshape(hidden_in.shape),
        out_qkv,
        mine[0],
        mine[1],
        sums[3],
        mine[2],
        mine[3],
        mine[4],
        out_up.reshape(shard, blocks * width),
        mine[8 : 8 + blocks].reshape(blocks * shard),
        sums[4 + blocks :].reshape(blocks * shard, width),
        mine[5],
        mine[6],
        mine[7],
    )


def solution(mesh):
    row, vector, slot = P("fsdp", None), P("fsdp"), P(None, "fsdp", "ctx", None)
    routed = dict(mesh.shape) == {"ctx": 8, "fsdp": 4}
    return jax.shard_map(
        functools.partial(body, routed),
        mesh=mesh,
        in_specs=(
            slot, P(None, "fsdp"), slot, row, vector, vector, row, vector, vector, vector, row, vector, row, vector,
            vector, vector,
        ),
        out_specs=(
            slot, slot, row, vector, vector, row, vector, vector, vector, row, vector, row, vector, vector, vector,
        ),
        check_vma=False,
    )
```

```python
import functools

import jax
import jax.numpy as jnp
from jax import lax
from jax.experimental import pallas as pl
from jax.experimental.pallas import tpu as pltpu
from jax.sharding import PartitionSpec as P

HEADS = 16
HEAD_DIM = 64
EPS = 1e-05
NEG_FILL = -1e30
MESH = pl.DeviceIdType.MESH
F32 = jnp.float32
BF16 = jnp.bfloat16
VMEM = pltpu.VMEM
DMA = pltpu.SemaphoreType.DMA
VMEM_LIMIT = 62 * 1024 * 1024
CHUNKS = 12


def layer_norm(inputs, ln_gain, ln_shift):
    center = jnp.mean(inputs, axis=-1, keepdims=True)
    centered = inputs - center
    spread = jnp.mean(centered * centered, axis=-1, keepdims=True)
    return centered * lax.rsqrt(spread + EPS) * ln_gain + ln_shift


def rows_sum(matrix):
    return jnp.sum(matrix.astype(F32), axis=0)


def matmul(left_side, right_side):
    return jnp.dot(left_side, right_side, preferred_element_type=F32)


def dot_nt(a, b):
    return lax.dot_general(a, b, (((1,), (1,)), ((), ())), preferred_element_type=F32)


def dot_tn(a, b):
    return lax.dot_general(a, b, (((0,), (0,)), ((), ())), preferred_element_type=F32)


def place():
    d = lax.axis_index("ctx")
    z = lax.axis_index("fsdp")
    return d, d // 4, lax.rem(d // 2, 2), lax.rem(d, 2), z


def remote(src, dst, send, recv, device):
    return pltpu.make_async_remote_copy(
        src_ref=src, dst_ref=dst, send_sem=send, recv_sem=recv, device_id=device, device_id_type=MESH
    )


def greet(devices):
    barrier = pltpu.get_barrier_semaphore()
    for device in devices:
        pl.semaphore_signal(barrier, inc=1, device_id=device, device_id_type=MESH)
    pl.semaphore_wait(barrier, len(devices))


def swap_rows(d):
    return (lambda s: 2 * s + d // 4), (lambda i: 4 * lax.rem(d, 2) + i)


def head_lanes(width):
    return lax.broadcasted_iota(jnp.int32, (1, width), 1) // HEAD_DIM


def attend(q, k, v, length, block, put):
    slots = k.shape[0]
    key_pos = lax.broadcasted_iota(jnp.int32, (1, slots), 1)
    bias = jnp.where(key_pos < length, 0.0, NEG_FILL).astype(F32)
    width = k.shape[1]
    lanes = head_lanes(width)
    causal = lax.broadcasted_iota(jnp.int32, (block, block), 1) <= lax.broadcasted_iota(
        jnp.int32, (block, block), 0
    )
    for start in range(0, slots, block):
        stop = start + block
        q_block = q[start:stop, :]
        sums, levels = None, None
        for head in range(width // HEAD_DIM):
            q_head = jnp.where(lanes == head, q_block, jnp.zeros_like(q_block)) * jnp.asarray(HEAD_DIM**-0.5, BF16)
            scores = dot_nt(q_head, k[:stop, :]) + bias[:, :stop]
            last = jnp.where(causal, scores[:, start:], NEG_FILL)
            top = jnp.max(last, axis=1, keepdims=True)
            if start:
                top = jnp.maximum(top, jnp.max(scores[:, :start], axis=1, keepdims=True))
                scores = jnp.concatenate([scores[:, :start], last], axis=1)
            else:
                scores = last
            weights = jnp.exp(scores - top)
            total = jnp.sum(weights, axis=1, keepdims=True)
            mixed = matmul(weights.astype(BF16), v[:stop, :]) / total
            level = top + jnp.log(total)
            sums = mixed if sums is None else jnp.where(lanes == head, mixed, sums)
            level = jnp.broadcast_to(level, mixed.shape)
            levels = level if levels is None else jnp.where(lanes == head, level, levels)
        put(start, stop, sums, levels)


def lanes_of(index, width=128):
    return pl.ds(pl.multiple_of(index * width, width), width)


def attend_back(q, k, v, o, levels, dm, length, block, put_query, put_key):
    slots, width = k.shape
    key_pos = lax.broadcasted_iota(jnp.int32, (1, slots), 1)
    bias = jnp.where(key_pos < length, 0.0, NEG_FILL).astype(F32)
    lanes = head_lanes(width)
    causal = lax.broadcasted_iota(jnp.int32, (block, block), 1) <= lax.broadcasted_iota(
        jnp.int32, (block, block), 0
    )
    scale = jnp.asarray(HEAD_DIM**-0.5, BF16)
    for start in range(0, slots, block):
        stop = start + block
        q_block = q[start:stop, :] * scale
        d_block = dm[start:stop, :]
        product = d_block.astype(F32) * o[start:stop, :].astype(F32)
        q_turned, d_turned = q_block.T, d_block.T
        d_query, d_keys, d_values = None, [], []
        for head in range(width // HEAD_DIM):
            here = lanes == head
            q_head = jnp.where(here, q_block, jnp.zeros_like(q_block))
            d_head = jnp.where(here, d_block, jnp.zeros_like(d_block))
            total = jnp.sum(jnp.where(here, product, 0.0), axis=1, keepdims=True)
            level = levels[start:stop, head * HEAD_DIM : head * HEAD_DIM + 1]
            scores = dot_nt(q_head, k[:stop, :]) + bias[:, :stop]
            last = jnp.where(causal, scores[:, start:], NEG_FILL)
            scores = jnp.concatenate([scores[:, :start], last], axis=1) if start else last
            weights = jnp.exp(scores - level)
            d_weight = dot_nt(d_head, v[:stop, :]) - total
            d_score = (weights * d_weight).astype(BF16)
            part = matmul(d_score, k[:stop, :])
            d_query = part if d_query is None else jnp.where(here, part, d_query)
            cut = slice(head * HEAD_DIM, (head + 1) * HEAD_DIM)
            d_values.append(matmul(d_turned[cut, :], weights.astype(BF16)))
            d_keys.append(matmul(q_turned[cut, :], d_score))
        put_query(start, stop, d_query * (HEAD_DIM**-0.5))
        put_key(start, stop, jnp.concatenate(d_keys, axis=0), jnp.concatenate(d_values, axis=0))


HIDDEN_BLOCKS = 4
UP, DOWN = 4, 5
GATHER_OFFSETS = (0, 1, 2, 3, 5, 7, 8)
GATHER_DELAY = 5


def flat_rows(value):
    return value.reshape((-1, value.shape[-1]))


def forward_kernel(
    w_qkv, w_out, w_up, w_down, small, hidden, cotangent, lengths,
    kept, full, home_hbm, normed_hbm, branch_hbm, buf_hbm, mine_hbm, level_hbm, mixed_hbm, residual_hbm,
    dx, g_up, g_down, g_bias, output,
    rows, normed, branch, buf, mine, level_out, mixed_low, residual, land, small_land, qkv, turned, total, stage_up, stage_down,
    ld, kd, vs, vr, zs, zr, xs, xr, cs, cr, hs, hr, es, er, ek, fs, fr, fk, us, ds_, os_,
):
    d, y, x, c, z = place()
    x_nb, y_nb, c_nb = (d + 2 - 4 * x, z), (d + 4 - 8 * y, z), (d + 1 - 2 * c, z)
    line = [(d, lax.rem(z + k, 4)) for k in (1, 2, 3)]
    width = full.shape[1]
    shard = width // 4
    half = normed.shape[0]
    pairs = mine.shape[1] // 128
    length = lengths[d // 4, lax.rem(d // 2, 2)]

    def own(chunk):
        copies = []
        if chunk < 3:
            copies.append((w_qkv.at[:, :, :, :, :, chunk * width : (chunk + 1) * width], land.at[chunk, z]))
        elif chunk == 3:
            copies.append((w_out, land.at[chunk, z]))
        elif chunk % 2 == UP % 2:
            j = (chunk - UP) // 2
            for i in range(4):
                low = i * width + j * shard
                copies.append(
                    (
                        w_up.at[:, :, :, :, :, low : low + shard],
                        land.at[chunk, z, :, :, :, :, :, i * shard : (i + 1) * shard],
                    )
                )
        else:
            copies.append((w_down.at[(chunk - DOWN) // 2], land.at[chunk, z]))
        return [pltpu.make_async_copy(a, b, ld.at[chunk, i]) for i, (a, b) in enumerate(copies)]

    for chunk in range(CHUNKS):
        for copy in own(chunk):
            copy.start()

    greet([(lax.rem(d + k, 8), z) for k in range(1, 8)] + line)

    goes, comes = swap_rows(d)

    def row_copy(ref, a, s):
        return remote(ref.at[s], rows.at[a, lax.rem(d, 4)], hs.at[a, s], hr.at[a, lax.rem(d, 4)], (goes(s), z))

    def row_keep(ref, a, s):
        return pltpu.make_async_copy(ref.at[s], rows.at[a, lax.rem(d, 4)], hs.at[a, s])

    def row_recv(a, i):
        ref = rows.at[a, i]
        return remote(ref, ref, hs.at[a, i], hr.at[a, i], c_nb)

    def rows_start(ref, a):
        for s in range(4):
            @pl.when(goes(s) == d)
            def _():
                row_keep(ref, a, s).start()

            @pl.when(goes(s) != d)
            def _():
                row_copy(ref, a, s).start()

    def rows_wait(ref, a):
        for s in range(4):
            @pl.when(goes(s) == d)
            def _():
                row_keep(ref, a, s).wait()

            @pl.when(goes(s) != d)
            def _():
                row_copy(ref, a, s).wait_send()

            @pl.when(comes(s) != d)
            def _():
                row_recv(a, s).wait_recv()

    def small_copy(k):
        return remote(small, small_land.at[z], vs.at[k], vr.at[k], line[k])

    def small_recv(k):
        return remote(small, small_land.at[lax.rem(z + 3 - k, 4)], vs.at[k], vr.at[k], line[k])

    def z_copy(chunk, k, down):
        ref = land.at[chunk, z + k if down else z - k, y, x, c]
        target = (d, z - 1) if down else (d, z + 1)
        return remote(ref, ref, zs.at[chunk, down, k], zr.at[chunk, down, k], target)

    def z_recv(chunk, k, down):
        ref = land.at[chunk, z + 1 + k if down else z - 1 - k, y, x, c]
        return remote(ref, ref, zs.at[chunk, down, k], zr.at[chunk, down, k], x_nb)

    def z_each(chunk, k, act_on):
        @pl.when((z < 3) & (z >= k))
        def _():
            act_on(z_copy(chunk, k, 0))

        @pl.when((z > 0) & (z + k <= 3))
        def _():
            act_on(z_copy(chunk, k, 1))

    def z_start(chunk, k):
        z_each(chunk, k, lambda copy: copy.start())

    def z_wait(chunk, k):
        @pl.when(z >= k + 1)
        def _():
            z_recv(chunk, k, 0).wait_recv()

        @pl.when(z + k + 1 <= 3)
        def _():
            z_recv(chunk, k, 1).wait_recv()

    def first(chunk, i, axis):
        ref = land.at[chunk, lax.rem(z + 1 + i, 4), y, x, c, axis]
        return remote(ref, ref, xs.at[chunk, 0, axis, i], xr.at[chunk, 0, axis, i], y_nb if axis else x_nb)

    def first_recv(chunk, i, axis):
        piece = lax.rem(z + 1 + i, 4)
        ref = land.at[chunk, piece, 1 - y, x, c, 1] if axis else land.at[chunk, piece, y, 1 - x, c, 0]
        return remote(ref, ref, xs.at[chunk, 0, axis, i], xr.at[chunk, 0, axis, i], y_nb if axis else x_nb)

    def second(chunk, i, axis):
        piece = lax.rem(z + 1 + i, 4)
        ref = land.at[chunk, piece, :, x, c, 1] if axis else land.at[chunk, piece, y, :, c, 0]
        return remote(ref, ref, xs.at[chunk, 1, axis, i], xr.at[chunk, 1, axis, i], x_nb if axis else y_nb)

    def second_recv(chunk, i, axis):
        piece = lax.rem(z + 1 + i, 4)
        ref = land.at[chunk, piece, :, 1 - x, c, 1] if axis else land.at[chunk, piece, 1 - y, :, c, 0]
        return remote(ref, ref, xs.at[chunk, 1, axis, i], xr.at[chunk, 1, axis, i], x_nb if axis else y_nb)

    def across(chunk, i, core):
        ref = land.at[chunk, lax.rem(z + 1 + i, 4), :, :, core]
        return remote(ref, ref, cs.at[chunk, i], cr.at[chunk, i], c_nb)

    def stage0(chunk):
        for index in range(CHUNKS):
            @pl.when(chunk == index)
            def _():
                for copy in own(index):
                    copy.wait()

        z_start(chunk, 0)

    def stage1(chunk):
        z_wait(chunk, 0)
        z_start(chunk, 1)

    def stage2(chunk):
        z_wait(chunk, 1)
        z_start(chunk, 2)

    def stage3(chunk):
        z_wait(chunk, 2)
        for i in range(3):
            for axis in range(2):
                first(chunk, i, axis).start()

    def stage4(chunk):
        for i in range(3):
            for axis in range(2):
                first_recv(chunk, i, axis).wait_recv()
        for i in range(3):
            for axis in range(2):
                second(chunk, i, axis).start()

    def stage5(chunk):
        for i in range(3):
            for axis in range(2):
                second_recv(chunk, i, axis).wait_recv()
        for i in range(3):
            across(chunk, i, c).start()

    def stage6(chunk):
        for i in range(3):
            across(chunk, i, 1 - c).wait_recv()
        for i in range(3):
            across(chunk, i, c).wait_send()
            for axis in range(2):
                first(chunk, i, axis).wait_send()
                second(chunk, i, axis).wait_send()
        for k in range(3):
            z_each(chunk, k, lambda copy: copy.wait_send())

    stages = [stage0, stage1, stage2, stage3, stage4, stage5, stage6]

    def tick(step):
        for index in reversed(range(len(stages))):
            begun = step - GATHER_OFFSETS[index]
            chunk = begun - jnp.where(begun >= 3, GATHER_DELAY, 0)

            @pl.when((begun >= 0) & ((begun < 3) | (begun >= 3 + GATHER_DELAY)) & (chunk < CHUNKS))
            def _():
                stages[index](chunk)

    results = [
        pltpu.make_async_copy(a, b, os_.at[i])
        for i, (a, b) in enumerate(
            [
                (rows.at[0], home_hbm), (normed, normed_hbm), (buf, buf_hbm), (mine, mine_hbm),
                (level_out, level_hbm), (mixed_low, mixed_hbm), (residual, residual_hbm), (branch, branch_hbm),
            ]
        )
    ]

    rows_start(hidden, 0)
    for k in range(3):
        small_copy(k).start()
    small_land[z] = small[...]

    @pl.loop(0, 4)
    def _(step):
        tick(step)

    for k in range(3):
        small_recv(k).wait_recv()
    for i in range(4):
        full[:, i * shard : (i + 1) * shard] = small_land[i].astype(F32)
    rows_wait(hidden, 0)

    def vector(index):
        return full[index : index + 1, :]

    @pl.loop(0, 4)
    def _(i):
        part = layer_norm(rows[0, i].astype(F32), vector(3), vector(4))
        normed[lanes_of(i), :] = part.astype(BF16)
        tick(4 + i)

    @pl.loop(8, 11)
    def _(step):
        tick(step)

    rows_start(cotangent, 1)
    results[0].start()
    results[1].start()
    for chunk in range(3):
        pltpu.make_async_copy(land.at[chunk], kept.at[chunk], kd.at[chunk]).start()
    tile = 256
    for u in range(3):
        @pl.loop(0, width // tile)
        def _(n):
            cut = lanes_of(n, tile)
            part = matmul(normed[...], flat_rows(land[u, :, :, :, :, :, :, cut]))
            if u != 1:
                part += full[u // 2 : u // 2 + 1, cut]
            qkv[u, :, cut] = part.astype(BF16)

        tick(11 + u)

    def send(h):
        return remote(
            qkv.at[:, :, lanes_of((1 - c) * pairs + h)],
            buf.at[:, lanes_of(c, half), lanes_of(h)], es.at[h], er.at[h], c_nb,
        )

    def keep(h):
        return pltpu.make_async_copy(
            qkv.at[:, :, lanes_of(c * pairs + h)], buf.at[:, lanes_of(c, half), lanes_of(h)], ek.at[h]
        )

    def recv(h):
        ref = buf.at[:, lanes_of(1 - c, half), lanes_of(h)]
        return remote(ref, ref, es.at[h], er.at[h], c_nb)

    def send_back(h):
        return remote(
            mine.at[lanes_of(1 - c, half), lanes_of(h)], mixed_low.at[:, lanes_of(c * pairs + h)],
            fs.at[h], fr.at[h], c_nb,
        )

    def keep_back(h):
        return pltpu.make_async_copy(
            mine.at[lanes_of(c, half), lanes_of(h)], mixed_low.at[:, lanes_of(c * pairs + h)], fk.at[h]
        )

    def recv_back(h):
        ref = mixed_low.at[:, lanes_of((1 - c) * pairs + h)]
        return remote(ref, ref, fs.at[h], fr.at[h], c_nb)

    @pl.loop(0, pairs)
    def _(h):
        send(h).start()
        keep(h).start()

    @pl.loop(0, pairs)
    def _(h):
        keep(h).wait()
        recv(h).wait_recv()
        cut = lanes_of(h)

        def put(start, stop, mixed, level):
            level_out[start:stop, cut] = level
            mine[start:stop, cut] = mixed.astype(BF16)

        attend(buf.at[0, :, cut], buf.at[1, :, cut], buf.at[2, :, cut], length, 256, put)
        send_back(h).start()
        keep_back(h).start()
        tick(14 + h)

    @pl.loop(0, pairs)
    def _(h):
        keep_back(h).wait()
        recv_back(h).wait_recv()
        send(h).wait_send()
        send_back(h).wait_send()

    for i in range(2, 6):
        results[i].start()

    act, d_pre, normed2 = qkv.at[0], qkv.at[1], qkv.at[2]

    @pl.loop(0, width // tile)
    def _(n):
        cut = lanes_of(n, tile)
        part = matmul(mixed_low[...], flat_rows(land[3, :, :, :, :, :, :, cut]))
        residual[:, cut] = flat_rows(rows[0, :, :, cut]).astype(F32) + part + full[2:3, cut]

    pltpu.make_async_copy(land.at[3], kept.at[3], kd.at[3]).start()
    tick(18)
    rows_wait(cotangent, 1)

    @pl.loop(0, 4)
    def _(i):
        cut = lanes_of(i)
        normed2[cut, :] = layer_norm(residual[cut, :], vector(6), vector(7)).astype(BF16)
        position = c * half + i * 128 + lax.broadcasted_iota(jnp.int32, (128, 1), 0)
        d_out = jnp.where(position < length, rows[1, i].astype(F32), 0.0)
        branch[cut, :] = d_out.astype(BF16)

    results[6].start()
    results[7].start()

    total[...] = jnp.zeros_like(total)
    dx[...] = jnp.zeros_like(dx)
    turned[...] = normed2[...].T

    def put_up(j, n):
        cut = lanes_of(n, tile)
        return pltpu.make_async_copy(stage_up.at[:, cut], g_up.at[j, :, cut], us.at[n])

    def put_down(j, n):
        cut = lanes_of(n, tile)
        return pltpu.make_async_copy(stage_down.at[cut, :], g_down.at[j, cut, :], ds_.at[n])

    @pl.loop(0, HIDDEN_BLOCKS)
    def _(j):
        up, down = UP + 2 * j, DOWN + 2 * j

        @pl.loop(0, width // tile)
        def _(n):
            cut = lanes_of(n, tile)

            @pl.when(j > 0)
            def _():
                put_up(j, n).wait()
                put_down(j, n).wait()

            pre = matmul(normed2[...], flat_rows(land[up, :, :, :, :, :, :, cut])) + full[pl.ds(8 + j, 1), cut]
            cumulative = 0.5 + 0.5 * lax.erf(pre * (0.5**0.5))
            active = (pre * cumulative).astype(BF16)
            act[:, cut] = active
            slope = cumulative + pre * (jnp.exp(-0.5 * pre * pre) * 0.3989422804014327)
            low = (dot_nt(branch[...], flat_rows(land[down, n])) * slope).astype(BF16)
            d_pre[:, cut] = low
            g_bias[pl.ds(j, 1), cut] = jnp.sum(low.astype(F32), axis=0, keepdims=True)
            stage_down[cut, :] = matmul(active.T, branch[...]).astype(BF16)
            stage_up[:, cut] = matmul(turned[...], low).astype(BF16)
            put_up(j, n).start()
            put_down(j, n).start()

        tick(19 + 2 * j)

        @pl.loop(0, width // tile)
        def _(n):
            cut = lanes_of(n, tile)
            total[:, cut] += matmul(act[...], flat_rows(land[down, :, :, :, :, :, :, cut]))
            dx[:, cut] += dot_nt(d_pre[...], flat_rows(land[up, n]))

        tick(20 + 2 * j)

    output[...] = (residual[...] + total[...] + full[5:6, :]).astype(BF16)
    for n in range(width // tile):
        put_up(0, n).wait()
        put_down(0, n).wait()
    for copy in results:
        copy.wait()
    for chunk in range(4):
        pltpu.make_async_copy(land.at[chunk], kept.at[chunk], kd.at[chunk]).wait()
    for k in range(3):
        small_copy(k).wait_send()


def forward(w_qkv, w_out, w_up, w_down, small, hidden, cotangent, lengths):
    shard, width = w_out.shape
    half = hidden.shape[0] * hidden.shape[1]
    slots, mine = 2 * half, width // 2
    pairs = mine // 128
    piece = (2, 2, 2, 2, shard // 16)
    vm, anywhere = pl.BlockSpec(memory_space=VMEM), pl.BlockSpec(memory_space=pl.ANY)
    shape = jax.ShapeDtypeStruct
    n = CHUNKS
    return pl.pallas_call(
        forward_kernel,
        out_shape=(
            shape((4, 4) + piece + (width,), BF16),
            shape((16, width), F32),
            shape(hidden.shape, BF16),
            shape((half, width), BF16),
            shape((half, width), BF16),
            shape((3, slots, mine), BF16),
            shape((slots, mine), BF16),
            shape((slots, mine), F32),
            shape((half, width), BF16),
            shape((half, width), F32),
            shape((half, width), F32),
            shape((HIDDEN_BLOCKS, width, width), BF16),
            shape((HIDDEN_BLOCKS, width, width), BF16),
            shape((8, width), F32),
            shape((half, width), BF16),
        ),
        in_specs=[anywhere] * 4 + [vm] + [anywhere] * 2 + [pl.BlockSpec(memory_space=pltpu.SMEM)],
        out_specs=(anywhere, vm) + (anywhere,) * 8 + (vm, anywhere, anywhere, vm, vm),
        scratch_shapes=[
            VMEM((2,) + hidden.shape, BF16),
            VMEM((half, width), BF16),
            VMEM((half, width), BF16),
            VMEM((3, slots, mine), BF16),
            VMEM((slots, mine), BF16),
            VMEM((slots, mine), F32),
            VMEM((half, width), BF16),
            VMEM((half, width), F32),
            VMEM((n, 4) + piece + (width,), BF16),
            VMEM((4,) + small.shape, BF16),
            VMEM((3, half, width), BF16),
            VMEM((width, half), BF16),
            VMEM((half, width), F32),
            VMEM((width, width), BF16),
            VMEM((width, width), BF16),
            DMA((n, 4)), DMA((4,)), DMA((3,)), DMA((3,)),
            DMA((n, 2, 3)), DMA((n, 2, 3)),
            DMA((n, 2, 2, 3)), DMA((n, 2, 2, 3)),
            DMA((n, 3)), DMA((n, 3)),
            DMA((2, 4)), DMA((2, 4)),
            DMA((pairs,)), DMA((pairs,)), DMA((pairs,)),
            DMA((pairs,)), DMA((pairs,)), DMA((pairs,)),
            DMA((4,)), DMA((4,)), DMA((8,)),
        ],
        compiler_params=pltpu.CompilerParams(
            collective_id=0, has_side_effects=True, vmem_limit_bytes=VMEM_LIMIT
        ),
        name="forward",
    )(
        w_qkv.reshape(piece + (3 * width,)),
        w_out.reshape(piece + (width,)),
        w_up.reshape(piece + (4 * width,)),
        w_down.reshape((HIDDEN_BLOCKS,) + piece + (width,)),
        small, hidden, cotangent, lengths,
    )


P_OFFSETS = (0, 1, 3, 5, 6, 7, 8, 9, 10, 11)
Q_OFFSETS = (0, 1, 3, 5, 7, 8, 9, 10, 11, 12)
LAST_STEP = 18
N_P, N_Q = 8, 4


def norm_back(x, upstream, gain):
    center = jnp.mean(x, axis=-1, keepdims=True)
    centered = x - center
    scale = lax.rsqrt(jnp.mean(centered * centered, axis=-1, keepdims=True) + EPS)
    hat = centered * scale
    t = upstream * gain
    back = scale * (t - jnp.mean(t, axis=-1, keepdims=True) - hat * jnp.mean(t * hat, axis=-1, keepdims=True))
    return back, jnp.sum(upstream * hat, axis=0, keepdims=True), jnp.sum(upstream, axis=0, keepdims=True)


def backward_kernel(
    kept, full, rows, normed, branch, buf, o_low, levels, mixed_low, residual, dx, g_up, g_down, g_bias, output,
    lengths,
    out, small_out, out_home, grad_home,
    acc, core_in, x_in, y_in, x_in2, y_in2, up_in, down_in, xq_in, yq_in, up_q, down_q, small_in,
    pair, pair_o, pair_l, dm, mine, turned, d_qkv, slot_a, slot_b, keep_f, work_f, d_attn, home_low, weight, stage,
    ls, cs, cr, s1, r1, s2, r2, zs, zr, gl, s3, r3, s4, r4, s5, r5, vs, vr, hs, hr,
    ps, ek, es, er, fk, fs, fr, ms, ws,
):
    d, y, x, c, z = place()
    x_nb, y_nb, c_nb = (d + 2 - 4 * x, z), (d + 4 - 8 * y, z), (d + 1 - 2 * c, z)
    line = [(d, lax.rem(z + k, 4)) for k in (1, 2, 3)]
    width = full.shape[1]
    half = d_attn.shape[0]
    pairs = dm.shape[1] // 128
    length = lengths[d // 4, lax.rem(d // 2, 2)]
    tile = 256

    def local(src, dst, sem):
        return pltpu.make_async_copy(src, dst, sem)

    loads = [
        local(residual, keep_f, ms.at[0]), local(dx, work_f, ms.at[1]), local(branch, slot_b, ms.at[2]),
        local(mixed_low, slot_a, ms.at[3]),
    ]
    for copy in loads:
        copy.start()
    local(kept.at[3], weight, ws).start()
    greet([(lax.rem(d + k, 8), z) for k in range(1, 8)] + line)

    comes, goes = swap_rows(d)

    def row_copy(src, dst, a, i):
        return remote(src(i), dst.at[d // 2], hs.at[a, i], hr.at[a, d // 2], (goes(i), z))

    def row_keep(src, dst, a, i):
        return local(src(i), dst.at[d // 2], hs.at[a, i])

    def row_recv(dst, a, s):
        return remote(dst.at[s], dst.at[s], hs.at[a, s], hr.at[a, s], c_nb)

    def rows_start(src, dst, a):
        for i in range(4):
            @pl.when(goes(i) == d)
            def _():
                row_keep(src, dst, a, i).start()

            @pl.when(goes(i) != d)
            def _():
                row_copy(src, dst, a, i).start()

    def rows_wait(src, dst, a):
        for i in range(4):
            @pl.when(goes(i) == d)
            def _():
                row_keep(src, dst, a, i).wait()

            @pl.when(goes(i) != d)
            def _():
                row_copy(src, dst, a, i).wait_send()

            @pl.when(comes(i) != d)
            def _():
                row_recv(dst, a, i).wait_recv()

    def output_block(i):
        return output.at[i]

    def grad_block(i):
        return home_low.at[i * 128 : (i + 1) * 128, :]

    def load(ref, chunk, slot):
        return local(ref.at[chunk, :, :, :, c], acc.at[slot], ls.at[slot])

    def core_send(ref, slot, into):
        return remote(ref, core_in.at[into], cs.at[slot], cr.at[slot], c_nb)

    def down_send(k):
        return core_send(g_down.at[k, :, :, :, 1 - c], k, k)

    def up_send(k):
        return core_send(g_up.at[k, :, :, :, 1 - c], N_P + k, 5 + k)

    def stage_send(slot, into):
        return core_send(stage, slot, into)

    def core_add(slot, into):
        stage_send(slot, into).wait_recv()
        for piece in range(4):
            acc[slot, piece] += core_in[into, piece]

    def x1(k):
        return remote(acc.at[k, :, :, 1 - x, 0], x_in.at[k], s1.at[k, 0], r1.at[k, 0], x_nb)

    def y1(k):
        return remote(acc.at[k, :, 1 - y, :, 1], y_in.at[k], s1.at[k, 1], r1.at[k, 1], y_nb)

    def y2(k):
        return remote(acc.at[k, :, 1 - y, x, 0], y_in2.at[k], s2.at[k, 0], r2.at[k, 0], y_nb)

    def x2(k):
        return remote(acc.at[k, :, y, 1 - x, 1], x_in2.at[k], s2.at[k, 1], r2.at[k, 1], x_nb)

    def qx1(k):
        return remote(acc.at[N_P + k, z, :, 1 - x, 0], xq_in.at[k, 0:2], s1.at[N_P + k, 0], r1.at[N_P + k, 0], x_nb)

    def qy1(k):
        return remote(acc.at[N_P + k, z, 1 - y, :, 1], yq_in.at[k, 0:2], s1.at[N_P + k, 1], r1.at[N_P + k, 1], y_nb)

    def qy2(k):
        return remote(acc.at[N_P + k, z, 1 - y, x, 0], yq_in.at[k, 2], s2.at[N_P + k, 0], r2.at[N_P + k, 0], y_nb)

    def qx2(k):
        return remote(acc.at[N_P + k, z, y, 1 - x, 1], xq_in.at[k, 2], s2.at[N_P + k, 1], r2.at[N_P + k, 1], x_nb)

    def p_up(k, i):
        return remote(acc.at[k, z + 3 - i, y, x], up_in.at[k, i], zs.at[k, 0, i], zr.at[k, 0, i], (d, z + 1))

    def p_down(k, i):
        return remote(acc.at[k, z - 3 + i, y, x], down_in.at[k, i], zs.at[k, 1, i], zr.at[k, 1, i], (d, z - 1))

    def q_up(k, i):
        return remote(
            acc.at[N_P + k, z + 3 - i], up_q.at[k, i], zs.at[N_P + k, 0, i], zr.at[N_P + k, 0, i], (d, z + 1)
        )

    def q_down(k, i):
        return remote(
            acc.at[N_P + k, z - 3 + i], down_q.at[k, i], zs.at[N_P + k, 1, i], zr.at[N_P + k, 1, i], (d, z - 1)
        )

    def z_each(up, down, k, i, act):
        @pl.when((z < 3) & (z <= i))
        def _():
            act(up(k, i))

        @pl.when((z > 0) & (z >= 3 - i))
        def _():
            act(down(k, i))

    def z_send(up, down, k, i):
        z_each(up, down, k, i, lambda copy: copy.start())

    def z_add(up_ref, down_ref, k, base, i, add_up, add_down):
        @pl.when((z >= 1) & (z - 1 <= i))
        def _():
            ref = up_ref.at[k, i]
            remote(ref, ref, zs.at[base + k, 0, i], zr.at[base + k, 0, i], c_nb).wait_recv()
            add_up(k, i)

        @pl.when((z <= 2) & (z + 1 >= 3 - i))
        def _():
            ref = down_ref.at[k, i]
            remote(ref, ref, zs.at[base + k, 1, i], zr.at[base + k, 1, i], c_nb).wait_recv()
            add_down(k, i)

    def p_add_up(k, i):
        acc[k, z + 2 - i, y, x] += up_in[k, i]

    def p_add_down(k, i):
        acc[k, z - 2 + i, y, x] += down_in[k, i]

    def q_add_up(k, i):
        acc[N_P + k, z + 2 - i] += up_q[k, i]

    def q_add_down(k, i):
        acc[N_P + k, z - 2 + i] += down_q[k, i]

    def g0(k):
        return local(acc.at[k, z, y, x], out.at[k, y, x, c], gl.at[k])

    def g1(k, axis):
        return remote(
            acc.at[k, z, y, x, axis], out.at[k, y, x, c, axis], s3.at[k, axis], r3.at[k, axis],
            y_nb if axis else x_nb,
        )

    def g1_recv(k, axis):
        ref = out.at[k, 1 - y, x, c, 1] if axis else out.at[k, y, 1 - x, c, 0]
        return remote(ref, ref, s3.at[k, axis], r3.at[k, axis], y_nb if axis else x_nb)

    def g2(k, axis):
        ref = out.at[k, :, x, c, 1] if axis else out.at[k, y, :, c, 0]
        return remote(ref, ref, s4.at[k, axis], r4.at[k, axis], x_nb if axis else y_nb)

    def g2_recv(k, axis):
        ref = out.at[k, :, 1 - x, c, 1] if axis else out.at[k, 1 - y, :, c, 0]
        return remote(ref, ref, s4.at[k, axis], r4.at[k, axis], x_nb if axis else y_nb)

    def g3(k, core):
        ref = out.at[k, :, :, core]
        return remote(ref, ref, s5.at[k], r5.at[k], c_nb)

    def spread1(k):
        g0(k).start()
        g1(k, 0).start()
        g1(k, 1).start()

    def spread2(k):
        g0(k).wait()
        for axis in range(2):
            g1_recv(k, axis).wait_recv()
        for axis in range(2):
            g2(k, axis).start()

    def spread3(k):
        for axis in range(2):
            g2_recv(k, axis).wait_recv()
        g3(k, c).start()

    def spread4(k):
        g3(k, 1 - c).wait_recv()
        g3(k, c).wait_send()
        for axis in range(2):
            g1(k, axis).wait_send()
            g2(k, axis).wait_send()

    def p0(k):
        @pl.when(k < 4)
        def _():
            down_send(k).start()
            load(g_down, k, k).start()

    def p1(k):
        @pl.when(k < 4)
        def _():
            load(g_down, k, k).wait()

        core_add(k, jnp.where(k >= 5, k - 5, k))
        x1(k).start()
        y1(k).start()

    def p2(k):
        x1(k).wait_recv()
        y1(k).wait_recv()
        acc[k, :, :, x, 0] += x_in[k]
        acc[k, :, y, :, 1] += y_in[k]
        y2(k).start()
        x2(k).start()

    def p3(k):
        y2(k).wait_recv()
        x2(k).wait_recv()
        acc[k, :, y, x, 0] += y_in2[k]
        acc[k, :, y, x, 1] += x_in2[k]
        z_send(p_up, p_down, k, 0)

    def p4(k):
        z_add(up_in, down_in, k, 0, 0, p_add_up, p_add_down)
        z_send(p_up, p_down, k, 1)

    def p5(k):
        z_add(up_in, down_in, k, 0, 1, p_add_up, p_add_down)
        z_send(p_up, p_down, k, 2)

    def p6(k):
        z_add(up_in, down_in, k, 0, 2, p_add_up, p_add_down)
        spread1(k)

    def p9(k):
        spread4(k)

        @pl.when(k < 4)
        def _():
            down_send(k).wait_send()

        for copy in (x1(k), y1(k), x2(k), y2(k)):
            copy.wait_send()
        for i in range(3):
            z_each(p_up, p_down, k, i, lambda copy: copy.wait_send())

    def q0(k):
        up_send(k).start()
        load(g_up, k, N_P + k).start()

    def q1(k):
        load(g_up, k, N_P + k).wait()
        core_add(N_P + k, 5 + k)
        z_send(q_up, q_down, k, 0)

    def q2(k):
        z_add(up_q, down_q, k, N_P, 0, q_add_up, q_add_down)
        z_send(q_up, q_down, k, 1)

    def q3(k):
        z_add(up_q, down_q, k, N_P, 1, q_add_up, q_add_down)
        z_send(q_up, q_down, k, 2)

    def q4(k):
        z_add(up_q, down_q, k, N_P, 2, q_add_up, q_add_down)
        qx1(k).start()
        qy1(k).start()

    def q5(k):
        qx1(k).wait_recv()
        qy1(k).wait_recv()
        acc[N_P + k, z, :, x, 0] += xq_in[k, 0:2]
        acc[N_P + k, z, y, :, 1] += yq_in[k, 0:2]
        qy2(k).start()
        qx2(k).start()

    def q6(k):
        qy2(k).wait_recv()
        qx2(k).wait_recv()
        acc[N_P + k, z, y, x, 0] += yq_in[k, 2]
        acc[N_P + k, z, y, x, 1] += xq_in[k, 2]
        spread1(N_P + k)

    def q9(k):
        spread4(N_P + k)
        up_send(k).wait_send()
        for copy in (qx1(k), qy1(k), qx2(k), qy2(k)):
            copy.wait_send()
        for i in range(3):
            z_each(q_up, q_down, k, i, lambda copy: copy.wait_send())

    p_stages = [p0, p1, p2, p3, p4, p5, p6, spread2, spread3, p9]
    q_stages = [
        q0, q1, q2, q3, q4, q5, q6, lambda k: spread2(N_P + k), lambda k: spread3(N_P + k), q9,
    ]

    def tick(step):
        step = jnp.asarray(step, jnp.int32)
        for index in reversed(range(10)):
            q_begun = step - Q_OFFSETS[index]

            @pl.when((q_begun == 0) | ((q_begun >= 0) & (q_begun < 2 * N_Q - 1) & (lax.rem(q_begun + 64, 2) == 1)))
            def _():
                q_stages[index]((q_begun + 1) // 2)

            begun = step - P_OFFSETS[index]

            @pl.when((begun >= 0) & (begun < N_P))
            def _():
                p_stages[index](begun)

    tick(0)
    rows_start(output_block, out_home, 0)

    for copy in loads:
        copy.wait()
    small_out[0] = jnp.zeros_like(small_out[0])
    small_out[0, 8:12, :] = g_bias[0:4, :]

    def add_small(index, value):
        small_out[0, index : index + 1, :] += value

    @pl.loop(0, 4)
    def _(i):
        cut = lanes_of(i)
        d_out = slot_b[cut, :].astype(F32)
        back, gain, shift = norm_back(keep_f[cut, :], work_f[cut, :], full[6:7, :])
        d_residual = d_out + back
        keep_f[cut, :] = d_residual
        low = d_residual.astype(BF16)
        d_attn[cut, :] = low
        add_small(2, jnp.sum(low.astype(F32), axis=0, keepdims=True))
        add_small(5, jnp.sum(d_out, axis=0, keepdims=True))
        add_small(6, gain)
        add_small(7, shift)

    tick(1)

    def put_gradient(slot, cut, value):
        value = value.astype(BF16).reshape(4, 2, 2, 2, 2, 16, tile)
        even, odd = value[:, :, :, 0], value[:, :, :, 1]
        first = c == 0
        acc[slot, :, :, :, :, :, cut] = jnp.where(first, even, odd)
        stage[:, :, :, :, :, cut] = jnp.where(first, odd, even)

    for i in range(2):
        d_qkv[0, :, i * half : (i + 1) * half] = slot_a[:, i * half : (i + 1) * half].T

    @pl.loop(0, width // tile)
    def _(n):
        cut = lanes_of(n, tile)
        halves = [matmul(d_qkv[0, :, i * half : (i + 1) * half], d_attn[:, cut]) for i in range(2)]
        put_gradient(4, cut, jnp.concatenate(halves, axis=0))

    stage_send(4, 4).start()
    local(kept.at[3], weight, ws).wait()

    @pl.loop(0, width // tile)
    def _(n):
        cut = lanes_of(n, tile)
        home_low[:, cut] = dot_nt(d_attn[...], flat_rows(weight[n])).astype(BF16)

    local(kept.at[0], weight, ws).start()
    home_rows = local(rows, slot_b, ms.at[2])
    normed_rows = local(normed, slot_a, ms.at[3])
    home_rows.start()
    normed_rows.start()

    def pair_loads(h):
        slot = lax.rem(h, 2)
        cut = lanes_of(h)
        return [
            local(buf.at[:, :, cut], pair.at[slot], ps.at[slot, 0]),
            local(o_low.at[:, cut], pair_o.at[slot], ps.at[slot, 1]),
            local(levels.at[:, cut], pair_l.at[slot], ps.at[slot, 2]),
        ]

    def send(h):
        return remote(
            home_low.at[:, lanes_of((1 - c) * pairs + h)], dm.at[lanes_of(c, half), lanes_of(h)],
            es.at[h], er.at[h], c_nb,
        )

    def keep(h):
        return local(home_low.at[:, lanes_of(c * pairs + h)], dm.at[lanes_of(c, half), lanes_of(h)], ek.at[h])

    def recv(h):
        ref = dm.at[lanes_of(1 - c, half), lanes_of(h)]
        return remote(ref, ref, es.at[h], er.at[h], c_nb)

    def send_back(h):
        return remote(
            mine.at[lax.rem(h, 2), :, lanes_of(1 - c, half), :], d_qkv.at[:, :, lanes_of(c * pairs + h)],
            fs.at[h], fr.at[h], c_nb,
        )

    def keep_back(h):
        return local(
            mine.at[lax.rem(h, 2), :, lanes_of(c, half), :], d_qkv.at[:, :, lanes_of(c * pairs + h)], fk.at[h]
        )

    def recv_back(h):
        ref = d_qkv.at[:, :, lanes_of((1 - c) * pairs + h)]
        return remote(ref, ref, fs.at[h], fr.at[h], c_nb)

    for copy in pair_loads(0):
        copy.start()

    @pl.loop(0, pairs)
    def _(h):
        send(h).start()
        keep(h).start()

    tick(2)

    @pl.loop(0, pairs)
    def _(h):
        for copy in pair_loads(h):
            copy.wait()

        @pl.when(h + 1 < pairs)
        def _():
            for copy in pair_loads(h + 1):
                copy.start()

        keep(h).wait()
        recv(h).wait_recv()

        @pl.when(h >= 2)
        def _():
            send_back(h - 2).wait_send()
            keep_back(h - 2).wait()

        turned[...] = jnp.zeros_like(turned)
        slot = lax.rem(h, 2)

        def put_query(start, stop, value):
            mine[slot, 0, start:stop, :] = value.astype(BF16)

        def put_key(start, stop, d_key, d_value):
            turned[0, :, :stop] += d_key
            turned[1, :, :stop] += d_value

        attend_back(
            pair.at[slot, 0], pair.at[slot, 1], pair.at[slot, 2], pair_o.at[slot], pair_l.at[slot],
            dm.at[:, lanes_of(h)], length, 256, put_query, put_key,
        )
        mine[slot, 1] = turned[0].T.astype(BF16)
        mine[slot, 2] = turned[1].T.astype(BF16)
        send_back(h).start()
        keep_back(h).start()
        tick(jnp.where(lax.rem(h, 2) == 1, 3 + h // 2, -1000))

    @pl.loop(0, pairs)
    def _(h):
        recv_back(h).wait_recv()
        send(h).wait_send()

    for h in range(pairs - 2, pairs):
        send_back(h).wait_send()
        keep_back(h).wait()
    home_rows.wait()
    normed_rows.wait()

    dm[...] = slot_a[...].T
    for u in range(3):
        stage_send(4 + u, 4 if u == 0 else u - 1).wait_send()

        @pl.loop(0, width // tile)
        def _(n):
            cut = lanes_of(n, tile)
            put_gradient(5 + u, cut, matmul(dm[...], d_qkv[u, :, cut]))

        stage_send(5 + u, u).start()
        local(kept.at[u], weight, ws).wait()

        @pl.loop(0, width // tile)
        def _(n):
            cut = lanes_of(n, tile)
            part = dot_nt(d_qkv[u], flat_rows(weight[n]))
            work_f[:, cut] = part if u == 0 else work_f[:, cut] + part

        if u < 2:
            local(kept.at[u + 1], weight, ws).start()
        if u != 1:
            add_small(u // 2, jnp.sum(d_qkv[u].astype(F32), axis=0, keepdims=True))
        tick(5 + u)

    @pl.loop(0, 4)
    def _(i):
        cut = lanes_of(i)
        back, gain, shift = norm_back(slot_b[cut, :].astype(F32), work_f[cut, :], full[3:4, :])
        home_low[cut, :] = (keep_f[cut, :] + back).astype(BF16)
        add_small(3, gain)
        add_small(4, shift)

    rows_start(grad_block, grad_home, 1)

    def vector_copy(step):
        nb = (c_nb, x_nb, y_nb)[step]
        return remote(small_out.at[step], small_in.at[step], vs.at[step], vr.at[step], nb)

    for step in range(3):
        vector_copy(step).start()
        tick(8 + step)
        vector_copy(step).wait()
        small_out[step + 1] = small_out[step] + small_in[step]
    copies = [remote(small_out.at[3], small_in.at[3 + k], vs.at[3 + k], vr.at[3 + k], line[k]) for k in range(3)]
    for copy in copies:
        copy.start()

    @pl.loop(11, LAST_STEP + 1)
    def _(step):
        tick(step)

    for copy in copies:
        copy.wait()
    small_out[4] = small_out[3] + small_in[3] + small_in[4] + small_in[5]
    stage_send(7, 2).wait_send()
    rows_wait(output_block, out_home, 0)
    rows_wait(grad_block, grad_home, 1)


def backward(
    kept, full, rows, normed, branch, buf, o_low, levels, mixed_low, residual, dx, g_up, g_down, g_bias, output, lengths
):
    half, width = normed.shape
    slots, lanes = o_low.shape
    pairs = lanes // 128
    piece, n = 16, N_P + N_Q
    vm, anywhere = pl.BlockSpec(memory_space=VMEM), pl.BlockSpec(memory_space=pl.ANY)
    shape = jax.ShapeDtypeStruct
    block = (4, 2, 2, 2, 2, piece, width)
    home = (4, half // 4, width)
    vectors = (16, width)
    out, small_out, out_home, grad_home = pl.pallas_call(
        backward_kernel,
        out_shape=(
            shape((n, 2, 2, 2, 2, piece, width), BF16),
            shape((5,) + vectors, F32),
            shape(home, BF16),
            shape(home, BF16),
        ),
        in_specs=[anywhere, vm] + [anywhere] * 11 + [vm, anywhere, pl.BlockSpec(memory_space=pltpu.SMEM)],
        out_specs=(anywhere, vm, anywhere, anywhere),
        scratch_shapes=[
            VMEM((n, 4, 2, 2, 2, piece, width), BF16),
            VMEM((9, 4, 2, 2, 2, piece, width), BF16),
            VMEM((N_P, 4, 2, piece, width), BF16),
            VMEM((N_P, 4, 2, piece, width), BF16),
            VMEM((N_P, 4, piece, width), BF16),
            VMEM((N_P, 4, piece, width), BF16),
            VMEM((N_P, 3, 2, piece, width), BF16),
            VMEM((N_P, 3, 2, piece, width), BF16),
            VMEM((N_Q, 3, piece, width), BF16),
            VMEM((N_Q, 3, piece, width), BF16),
            VMEM((N_Q, 3, 2, 2, 2, piece, width), BF16),
            VMEM((N_Q, 3, 2, 2, 2, piece, width), BF16),
            VMEM((6,) + vectors, F32),
            VMEM((2, 3, slots, 128), BF16),
            VMEM((2, slots, 128), BF16),
            VMEM((2, slots, 128), F32),
            VMEM((slots, lanes), BF16),
            VMEM((2, 3, slots, 128), BF16),
            VMEM((2, 128, slots), F32),
            VMEM((3, half, width), BF16),
            VMEM((half, width), BF16),
            VMEM((half, width), BF16),
            VMEM((half, width), F32),
            VMEM((half, width), F32),
            VMEM((half, width), BF16),
            VMEM((half, width), BF16),
            VMEM(block, BF16),
            VMEM((4, 2, 2, 2, piece, width), BF16),
            DMA((n,)), DMA((n,)), DMA((n,)),
            DMA((n, 2)), DMA((n, 2)), DMA((n, 2)), DMA((n, 2)),
            DMA((n, 2, 3)), DMA((n, 2, 3)), DMA((n,)),
            DMA((n, 2)), DMA((n, 2)), DMA((n, 2)), DMA((n, 2)),
            DMA((n,)), DMA((n,)), DMA((6,)), DMA((6,)),
            DMA((2, 4)), DMA((2, 4)),
            DMA((2, 3)),
            DMA((pairs,)), DMA((pairs,)), DMA((pairs,)),
            DMA((pairs,)), DMA((pairs,)), DMA((pairs,)),
            DMA((4,)), DMA,
        ],
        compiler_params=pltpu.CompilerParams(
            collective_id=1, has_side_effects=True, vmem_limit_bytes=VMEM_LIMIT
        ),
        name="backward",
    )(
        kept, full, rows.reshape(half, width), normed, branch, buf, o_low, levels, mixed_low, residual, dx,
        g_up.reshape((N_Q,) + block), g_down.reshape((4,) + block), g_bias, output.reshape(home), lengths,
    )
    return out.reshape(n, 16 * piece, width), small_out[4], out_home, grad_home


def feed_kernel(x, d_out, w_up, w_down, bias, y, dx, g_up, g_down, g_bias, x_turned, act, d_pre):
    tile = 256
    hidden = w_up.shape[2]

    @pl.when(pl.program_id(0) == 0)
    def _():
        y[...] = jnp.zeros_like(y)
        dx[...] = jnp.zeros_like(dx)
        x_turned[...] = x[...].T

    @pl.loop(0, hidden // tile)
    def _(n):
        cut = pl.ds(pl.multiple_of(n * tile, tile), tile)
        pre = matmul(x[...], w_up[0, :, cut]) + bias[0, :, cut].astype(F32)
        cumulative = 0.5 + 0.5 * lax.erf(pre * (0.5**0.5))
        active = (pre * cumulative).astype(BF16)
        act[:, cut] = active
        slope = cumulative + pre * (jnp.exp(-0.5 * pre * pre) * 0.3989422804014327)
        back = dot_nt(d_out[...], w_down[0, cut, :]) * slope
        low = back.astype(BF16)
        d_pre[:, cut] = low
        g_bias[0, :, cut] = jnp.sum(low.astype(F32), axis=0, keepdims=True)
        g_down[0, cut, :] = matmul(active.T, d_out[...]).astype(BF16)
        g_up[0, :, cut] = matmul(x_turned[...], low).astype(BF16)

    @pl.loop(0, y.shape[1] // tile)
    def _(n):
        cut = pl.ds(pl.multiple_of(n * tile, tile), tile)
        y[:, cut] += matmul(act[...], w_down[0, :, cut])
        dx[:, cut] += dot_nt(d_pre[...], w_up[0, cut, :])


def feed_forward(x, d_out, weights, bias, first_up, first_down, blocks):
    rows, width = x.shape
    hidden = weights.shape[2]
    whole = pl.BlockSpec((rows, width), lambda j: (0, 0))
    return pl.pallas_call(
        feed_kernel,
        grid=(blocks,),
        out_shape=(
            jax.ShapeDtypeStruct((rows, width), F32),
            jax.ShapeDtypeStruct((rows, width), F32),
            jax.ShapeDtypeStruct((blocks, width, hidden), BF16),
            jax.ShapeDtypeStruct((blocks, hidden, width), BF16),
            jax.ShapeDtypeStruct((blocks, 1, hidden), F32),
        ),
        in_specs=[
            whole,
            whole,
            pl.BlockSpec((1, width, hidden), lambda j: (first_up + j, 0, 0)),
            pl.BlockSpec((1, hidden, width), lambda j: (first_down + j, 0, 0)),
            pl.BlockSpec((1, 1, hidden), lambda j: (j, 0, 0)),
        ],
        out_specs=(
            whole,
            whole,
            pl.BlockSpec((1, width, hidden), lambda j: (j, 0, 0)),
            pl.BlockSpec((1, hidden, width), lambda j: (j, 0, 0)),
            pl.BlockSpec((1, 1, hidden), lambda j: (j, 0, 0)),
        ),
        scratch_shapes=[VMEM((width, rows), BF16), VMEM((rows, hidden), BF16), VMEM((rows, hidden), BF16)],
        compiler_params=pltpu.CompilerParams(
            dimension_semantics=("arbitrary",), vmem_limit_bytes=VMEM_LIMIT
        ),
        cost_estimate=pl.CostEstimate(
            flops=12 * blocks * rows * width * hidden,
            bytes_accessed=8 * blocks * width * hidden + 12 * rows * width,
            transcendentals=2 * blocks * rows * hidden,
        ),
        name="feed_forward",
    )(x, d_out, weights, weights, bias)


def finish_kernel(sums, qkv, out, up, down):
    width = out.shape[1]
    shard = width // 4
    out[...] = sums[4].astype(F32)
    for i in range(3):
        qkv[:, i * width : (i + 1) * width] = sums[5 + i].astype(F32)
    for j in range(4):
        down[j] = sums[j].astype(F32)
        value = sums[8 + j].astype(F32)
        for i in range(4):
            low = i * width + j * shard
            up[:, low : low + shard] = value[:, i * shard : (i + 1) * shard]


def finish(sums):
    n, rows, width = sums.shape
    tile = 32
    qkv, out, up, down = pl.pallas_call(
        finish_kernel,
        grid=(rows // tile,),
        out_shape=(
            jax.ShapeDtypeStruct((rows, 3 * width), F32),
            jax.ShapeDtypeStruct((rows, width), F32),
            jax.ShapeDtypeStruct((rows, 4 * width), F32),
            jax.ShapeDtypeStruct((4, rows, width), F32),
        ),
        in_specs=[pl.BlockSpec((n, tile, width), lambda i: (0, i, 0))],
        out_specs=(
            pl.BlockSpec((tile, 3 * width), lambda i: (i, 0)),
            pl.BlockSpec((tile, width), lambda i: (i, 0)),
            pl.BlockSpec((tile, 4 * width), lambda i: (i, 0)),
            pl.BlockSpec((4, tile, width), lambda i: (0, i, 0)),
        ),
        compiler_params=pltpu.CompilerParams(dimension_semantics=("arbitrary",), vmem_limit_bytes=32 * 1024 * 1024),
        name="finish",
    )(sums)
    return qkv, out, up, down.reshape(4 * rows, width)


def any_finish(sums):
    shard, width = sums.shape[1:]
    shards, blocks = width // shard, (sums.shape[0] - 4) // 2
    sums = sums.astype(F32)
    up = jnp.transpose(sums[4 : 4 + blocks].reshape(blocks, shard, shards, shard), (1, 2, 0, 3))
    return (
        jnp.transpose(sums[:3], (1, 0, 2)).reshape(shard, 3 * width),
        sums[3],
        up.reshape(shard, blocks * width),
        sums[4 + blocks :].reshape(blocks * shard, width),
    )


def any_gather(w_qkv, w_out, w_up, w_down, small):
    shard, width = w_out.shape
    shards, blocks = width // shard, w_up.shape[1] // width
    up_parts = jnp.transpose(w_up.reshape(shard, shards, blocks, shard), (2, 0, 1, 3)).reshape(blocks, shard, width)
    packed = jnp.concatenate(
        [
            jnp.transpose(w_qkv.reshape(shard, 3, width), (1, 0, 2)),
            w_out[None],
            up_parts,
            w_down.reshape(blocks, shard, width),
        ],
        axis=0,
    )
    return (
        lax.all_gather(packed, "fsdp", axis=1, tiled=True),
        lax.all_gather(small, "fsdp", axis=0, tiled=False),
    )


def any_reduce(parts, small):
    out = []
    for part in parts:
        mine = lax.psum_scatter(part, "fsdp", scatter_dimension=1, tiled=True)
        out.append(lax.psum(mine, "ctx"))
    return jnp.concatenate(out, axis=0), lax.psum(small, ("ctx", "fsdp"))


def any_forward(qkv, lengths):
    count = lengths.shape[0]
    qkv = qkv.reshape(3, count, -1, qkv.shape[2])
    wide = lax.all_to_all(qkv, "ctx", split_axis=3, concat_axis=2, tiled=True)
    wide = jnp.swapaxes(wide, 0, 1)

    def one(item):
        rows, length = item
        mixed, levels = [], []

        def put(start, stop, part, level):
            mixed.append(part)
            levels.append(level)

        attend(rows[0], rows[1], rows[2], length, rows.shape[1], put)
        return mixed[0], levels[0]

    mixed, levels = lax.map(one, (wide, lengths))
    low = lax.all_to_all(mixed.astype(BF16), "ctx", split_axis=1, concat_axis=2, tiled=True)
    return low.reshape(-1, low.shape[2]), wide, mixed, levels


def any_backward(dm_home, wide, mixed, levels, lengths):
    dm_home = dm_home.reshape(lengths.shape[0], -1, dm_home.shape[1])
    dm = lax.all_to_all(dm_home, "ctx", split_axis=2, concat_axis=1, tiled=True)

    def one(item):
        rows, part, level, upstream, length = item
        found = {}

        def put_query(start, stop, value):
            found[0] = value.astype(BF16)

        def put_key(start, stop, d_key, d_value):
            found[1], found[2] = d_key.T.astype(BF16), d_value.T.astype(BF16)

        attend_back(
            rows[0], rows[1], rows[2], part, level, upstream, length, rows.shape[1], put_query, put_key
        )
        return jnp.stack([found[0], found[1], found[2]])

    out = lax.map(one, (wide, mixed, levels, dm, lengths))
    out = lax.all_to_all(out, "ctx", split_axis=2, concat_axis=3, tiled=True)
    out = jnp.swapaxes(out, 0, 1)
    return out.reshape(3, -1, out.shape[3])


def any_layer(w_qkv, w_out, w_up, w_down, small, hidden_in, cotangent, flat_lengths):
    batch, seqs, slots, width = hidden_in.shape
    rows = batch * seqs * slots
    blocks = w_up.shape[1] // width
    weights, small_all = any_gather(w_qkv, w_out, w_up, w_down, small)
    position = lax.axis_index("ctx") * slots + jnp.arange(slots, dtype=jnp.int32)
    filled = (position[None, :] < flat_lengths[:, None]).astype(F32)
    small_all = jnp.transpose(small_all, (1, 0, 2)).reshape(16, width)
    full = small_all.astype(F32)
    full_q, full_v, full_bias_out, gain_one, shift_one, full_bias_down, gain_two, shift_two = [
        full[i] for i in range(8)
    ]
    full_up = small_all[8 : 8 + blocks].reshape(blocks, 1, width)
    flat_in = hidden_in.reshape(rows, width).astype(F32)
    normed = layer_norm(flat_in, gain_one, shift_one).astype(BF16)
    queries = (matmul(normed, weights[0]) + full_q).astype(BF16)
    key_rows = matmul(normed, weights[1]).astype(BF16)
    value_rows = (matmul(normed, weights[2]) + full_v).astype(BF16)
    qkv = jnp.stack([queries, key_rows, value_rows])
    mixed_low, wide, mixed, levels = any_forward(qkv, flat_lengths)
    residual = flat_in + matmul(mixed_low, weights[3]) + full_bias_out
    normed2 = layer_norm(residual, gain_two, shift_two).astype(BF16)
    d_out = cotangent.reshape(rows, width).astype(F32) * filled.reshape(rows, 1)
    fed, d_normed2, grad_up, grad_down, grad_bias_up = feed_forward(
        normed2, d_out.astype(BF16), weights, full_up, 4, 4 + blocks, blocks
    )
    output = (residual + fed + full_bias_down).astype(BF16)
    norm_pull_two = jax.vjp(layer_norm, residual, gain_two, shift_two)[1]
    d_resid_norm, grad_ln2_gain, grad_ln2_bias = norm_pull_two(d_normed2)
    d_residual = d_out + d_resid_norm
    d_attn = d_residual.astype(BF16)
    grad_out = dot_tn(mixed_low, d_attn).astype(BF16)
    d_mixed = dot_nt(d_attn, weights[3]).astype(BF16)
    d_qkv = any_backward(d_mixed, wide, mixed, levels, flat_lengths)
    grad_qkv = jnp.stack([dot_tn(normed, d_qkv[i]).astype(BF16) for i in range(3)])
    d_normed = sum(dot_nt(d_qkv[i], weights[i]) for i in range(3))
    norm_pull_one = jax.vjp(layer_norm, flat_in, gain_one, shift_one)[1]
    d_input_norm, grad_ln1_gain, grad_ln1_bias = norm_pull_one(d_normed)
    small_grads = jnp.stack(
        [
            rows_sum(d_qkv[0]),
            rows_sum(d_qkv[2]),
            rows_sum(d_attn),
            grad_ln1_gain,
            grad_ln1_bias,
            jnp.sum(d_out, axis=0),
            grad_ln2_gain,
            grad_ln2_bias,
        ]
        + [grad_bias_up[j, 0] for j in range(blocks)]
        + [jnp.zeros((width,), F32)] * (8 - blocks)
    )
    return output, d_residual + d_input_norm, [grad_qkv, grad_out[None], grad_up, grad_down], small_grads


def body(
    routed,
    hidden_in,
    lengths,
    cotangent,
    w_qkv,
    bias_q,
    bias_v,
    w_out,
    bias_out,
    ln1_gain,
    ln1_bias,
    w_up,
    bias_up,
    w_down,
    bias_down,
    ln2_gain,
    ln2_bias,
):
    batch, seqs, slots, width = hidden_in.shape
    count = batch * seqs
    rows = count * slots
    shard = w_qkv.shape[0]
    blocks = w_up.shape[1] // width
    vectors = [bias_q, bias_v, bias_out, ln1_gain, ln1_bias, bias_down, ln2_gain, ln2_bias]
    vectors += [bias_up[j * shard : (j + 1) * shard] for j in range(blocks)]
    which = lax.broadcasted_iota(jnp.int32, (16, shard), 0)
    small = jnp.zeros((16, shard), BF16)
    for i, vector in enumerate(vectors):
        small = jnp.where(which == i, vector[None, :], small)
    flat_lengths = lengths.reshape(count)
    if routed:
        *kept, output = forward(
            w_qkv, w_out, w_up, w_down, small,
            hidden_in.reshape(count, slots, width), cotangent.reshape(count, slots, width), lengths,
        )
        sums, small_sums, output, grad_hidden = backward(*kept, output, lengths)
        grad_hidden = grad_hidden.astype(F32)
        out_qkv, out_out, out_up, out_down = finish(sums)
    else:
        output, grad_hidden, parts, small_grads = any_layer(
            w_qkv, w_out, w_up, w_down, small, hidden_in, cotangent, flat_lengths
        )
        sums, small_sums = any_reduce(parts, small_grads)
        out_qkv, out_out, out_up, out_down = any_finish(sums)
    mine = lax.dynamic_slice_in_dim(small_sums, lax.axis_index("fsdp") * shard, shard, 1)
    return (
        output.reshape(hidden_in.shape),
        grad_hidden.reshape(hidden_in.shape),
        out_qkv,
        mine[0],
        mine[1],
        out_out,
        mine[2],
        mine[3],
        mine[4],
        out_up,
        mine[8 : 8 + blocks].reshape(blocks * shard),
        out_down,
        mine[5],
        mine[6],
        mine[7],
    )


def solution(mesh):
    row, vector, slot = P("fsdp", None), P("fsdp"), P(None, "fsdp", "ctx", None)
    routed = dict(mesh.shape) == {"ctx": 8, "fsdp": 4}
    return jax.shard_map(
        functools.partial(body, routed),
        mesh=mesh,
        in_specs=(
            slot, P(None, "fsdp"), slot, row, vector, vector, row, vector, vector, vector, row, vector, row, vector,
            vector, vector,
        ),
        out_specs=(
            slot, slot, row, vector, vector, row, vector, vector, vector, row, vector, row, vector, vector, vector,
        ),
        check_vma=False,
    )
```

```python
import functools

import jax
import jax.numpy as jnp
from jax import lax
from jax.experimental import pallas as pl
from jax.experimental.pallas import tpu as pltpu
from jax.sharding import PartitionSpec as P

HEADS = 16
HEAD_DIM = 64
EPS = 1e-05
NEG_FILL = -1e30
MESH = pl.DeviceIdType.MESH
F32 = jnp.float32
BF16 = jnp.bfloat16
VMEM = pltpu.VMEM
DMA = pltpu.SemaphoreType.DMA
VMEM_LIMIT = 62 * 1024 * 1024
CHUNKS = 12


def layer_norm(inputs, ln_gain, ln_shift):
    center = jnp.mean(inputs, axis=-1, keepdims=True)
    centered = inputs - center
    spread = jnp.mean(centered * centered, axis=-1, keepdims=True)
    return centered * lax.rsqrt(spread + EPS) * ln_gain + ln_shift


def rows_sum(matrix):
    return jnp.sum(matrix.astype(F32), axis=0)


def matmul(left_side, right_side):
    return jnp.dot(left_side, right_side, preferred_element_type=F32)


def dot_nt(a, b):
    return lax.dot_general(a, b, (((1,), (1,)), ((), ())), preferred_element_type=F32)


def dot_tn(a, b):
    return lax.dot_general(a, b, (((0,), (0,)), ((), ())), preferred_element_type=F32)


def place():
    d = lax.axis_index("ctx")
    z = lax.axis_index("fsdp")
    return d, d // 4, lax.rem(d // 2, 2), lax.rem(d, 2), z


def remote(src, dst, send, recv, device):
    return pltpu.make_async_remote_copy(
        src_ref=src, dst_ref=dst, send_sem=send, recv_sem=recv, device_id=device, device_id_type=MESH
    )


def greet(devices):
    barrier = pltpu.get_barrier_semaphore()
    for device in devices:
        pl.semaphore_signal(barrier, inc=1, device_id=device, device_id_type=MESH)
    pl.semaphore_wait(barrier, len(devices))


def swap_rows(d):
    return (lambda s: 2 * s + d // 4), (lambda i: 4 * lax.rem(d, 2) + i)


def head_lanes(width):
    return lax.broadcasted_iota(jnp.int32, (1, width), 1) // HEAD_DIM


def attend(q, k, v, length, block, put):
    slots = k.shape[0]
    key_pos = lax.broadcasted_iota(jnp.int32, (1, slots), 1)
    bias = jnp.where(key_pos < length, 0.0, NEG_FILL).astype(F32)
    width = k.shape[1]
    lanes = head_lanes(width)
    causal = lax.broadcasted_iota(jnp.int32, (block, block), 1) <= lax.broadcasted_iota(
        jnp.int32, (block, block), 0
    )
    for start in range(0, slots, block):
        stop = start + block
        q_block = q[start:stop, :]
        sums, levels = None, None
        for head in range(width // HEAD_DIM):
            q_head = jnp.where(lanes == head, q_block, jnp.zeros_like(q_block)) * jnp.asarray(HEAD_DIM**-0.5, BF16)
            scores = dot_nt(q_head, k[:stop, :]) + bias[:, :stop]
            last = jnp.where(causal, scores[:, start:], NEG_FILL)
            top = jnp.max(last, axis=1, keepdims=True)
            if start:
                top = jnp.maximum(top, jnp.max(scores[:, :start], axis=1, keepdims=True))
                scores = jnp.concatenate([scores[:, :start], last], axis=1)
            else:
                scores = last
            weights = jnp.exp(scores - top)
            total = jnp.sum(weights, axis=1, keepdims=True)
            mixed = matmul(weights.astype(BF16), v[:stop, :]) / total
            level = top + jnp.log(total)
            sums = mixed if sums is None else jnp.where(lanes == head, mixed, sums)
            level = jnp.broadcast_to(level, mixed.shape)
            levels = level if levels is None else jnp.where(lanes == head, level, levels)
        put(start, stop, sums, levels)


def lanes_of(index, width=128):
    return pl.ds(pl.multiple_of(index * width, width), width)


def attend_back(q, k, v, o, levels, dm, length, block, put_query, put_key):
    slots, width = k.shape
    key_pos = lax.broadcasted_iota(jnp.int32, (1, slots), 1)
    bias = jnp.where(key_pos < length, 0.0, NEG_FILL).astype(F32)
    lanes = head_lanes(width)
    causal = lax.broadcasted_iota(jnp.int32, (block, block), 1) <= lax.broadcasted_iota(
        jnp.int32, (block, block), 0
    )
    scale = jnp.asarray(HEAD_DIM**-0.5, BF16)
    for start in range(0, slots, block):
        stop = start + block
        q_block = q[start:stop, :] * scale
        d_block = dm[start:stop, :]
        product = d_block.astype(F32) * o[start:stop, :].astype(F32)
        q_turned, d_turned = q_block.T, d_block.T
        d_query, d_keys, d_values = None, [], []
        for head in range(width // HEAD_DIM):
            here = lanes == head
            q_head = jnp.where(here, q_block, jnp.zeros_like(q_block))
            d_head = jnp.where(here, d_block, jnp.zeros_like(d_block))
            total = jnp.sum(jnp.where(here, product, 0.0), axis=1, keepdims=True)
            level = levels[start:stop, head * HEAD_DIM : head * HEAD_DIM + 1]
            scores = dot_nt(q_head, k[:stop, :]) + bias[:, :stop]
            last = jnp.where(causal, scores[:, start:], NEG_FILL)
            scores = jnp.concatenate([scores[:, :start], last], axis=1) if start else last
            weights = jnp.exp(scores - level)
            d_weight = dot_nt(d_head, v[:stop, :]) - total
            d_score = (weights * d_weight).astype(BF16)
            part = matmul(d_score, k[:stop, :])
            d_query = part if d_query is None else jnp.where(here, part, d_query)
            cut = slice(head * HEAD_DIM, (head + 1) * HEAD_DIM)
            d_values.append(matmul(d_turned[cut, :], weights.astype(BF16)))
            d_keys.append(matmul(q_turned[cut, :], d_score))
        put_query(start, stop, d_query * (HEAD_DIM**-0.5))
        put_key(start, stop, jnp.concatenate(d_keys, axis=0), jnp.concatenate(d_values, axis=0))


HIDDEN_BLOCKS = 4
UP, DOWN = 4, 5
GATHER_OFFSETS = (0, 1, 2, 3, 6, 8, 9)
GATHER_DELAY = 4


def flat_rows(value):
    return value.reshape((-1, value.shape[-1]))


def forward_kernel(
    w_qkv, w_out, w_up, w_down, small, hidden, cotangent, lengths,
    kept, full, home_hbm, normed_hbm, branch_hbm, buf_hbm, mine_hbm, level_hbm, mixed_hbm, residual_hbm,
    dx, g_up, g_down, g_bias, output,
    rows, normed, branch, buf, mine, level_out, mixed_low, residual, land, small_land, qkv, turned, total, stage_up, stage_down,
    ld, kd, vs, vr, zs, zr, xs, xr, cs, cr, hs, hr, es, er, ek, fs, fr, fk, us, ds_, os_,
):
    d, y, x, c, z = place()
    x_nb, y_nb, c_nb = (d + 2 - 4 * x, z), (d + 4 - 8 * y, z), (d + 1 - 2 * c, z)
    line = [(d, lax.rem(z + k, 4)) for k in (1, 2, 3)]
    width = full.shape[1]
    shard = width // 4
    half = normed.shape[0]
    pairs = mine.shape[1] // 128
    length = lengths[d // 4, lax.rem(d // 2, 2)]

    def own(chunk):
        copies = []
        if chunk < 3:
            copies.append((w_qkv.at[:, :, :, :, :, chunk * width : (chunk + 1) * width], land.at[chunk, z]))
        elif chunk == 3:
            copies.append((w_out, land.at[chunk, z]))
        elif chunk % 2 == UP % 2:
            j = (chunk - UP) // 2
            for i in range(4):
                low = i * width + j * shard
                copies.append(
                    (
                        w_up.at[:, :, :, :, :, low : low + shard],
                        land.at[chunk, z, :, :, :, :, :, i * shard : (i + 1) * shard],
                    )
                )
        else:
            copies.append((w_down.at[(chunk - DOWN) // 2], land.at[chunk, z]))
        return [pltpu.make_async_copy(a, b, ld.at[chunk, i]) for i, (a, b) in enumerate(copies)]

    for chunk in range(CHUNKS):
        for copy in own(chunk):
            copy.start()

    greet([(lax.rem(d + k, 8), z) for k in range(1, 8)] + line)

    goes, comes = swap_rows(d)

    def row_copy(ref, a, s):
        return remote(ref.at[s], rows.at[a, lax.rem(d, 4)], hs.at[a, s], hr.at[a, lax.rem(d, 4)], (goes(s), z))

    def row_keep(ref, a, s):
        return pltpu.make_async_copy(ref.at[s], rows.at[a, lax.rem(d, 4)], hs.at[a, s])

    def row_recv(a, i):
        ref = rows.at[a, i]
        return remote(ref, ref, hs.at[a, i], hr.at[a, i], c_nb)

    def rows_start(ref, a):
        for s in range(4):
            @pl.when(goes(s) == d)
            def _():
                row_keep(ref, a, s).start()

            @pl.when(goes(s) != d)
            def _():
                row_copy(ref, a, s).start()

    def rows_wait(ref, a):
        for s in range(4):
            @pl.when(goes(s) == d)
            def _():
                row_keep(ref, a, s).wait()

            @pl.when(goes(s) != d)
            def _():
                row_copy(ref, a, s).wait_send()

            @pl.when(comes(s) != d)
            def _():
                row_recv(a, s).wait_recv()

    def small_copy(k):
        return remote(small, small_land.at[z], vs.at[k], vr.at[k], line[k])

    def small_recv(k):
        return remote(small, small_land.at[lax.rem(z + 3 - k, 4)], vs.at[k], vr.at[k], line[k])

    def z_copy(chunk, k, down):
        ref = land.at[chunk, z + k if down else z - k, y, x, c]
        target = (d, z - 1) if down else (d, z + 1)
        return remote(ref, ref, zs.at[chunk, down, k], zr.at[chunk, down, k], target)

    def z_recv(chunk, k, down):
        ref = land.at[chunk, z + 1 + k if down else z - 1 - k, y, x, c]
        return remote(ref, ref, zs.at[chunk, down, k], zr.at[chunk, down, k], x_nb)

    def z_each(chunk, k, act_on):
        @pl.when((z < 3) & (z >= k))
        def _():
            act_on(z_copy(chunk, k, 0))

        @pl.when((z > 0) & (z + k <= 3))
        def _():
            act_on(z_copy(chunk, k, 1))

    def z_start(chunk, k):
        z_each(chunk, k, lambda copy: copy.start())

    def z_wait(chunk, k):
        @pl.when(z >= k + 1)
        def _():
            z_recv(chunk, k, 0).wait_recv()

        @pl.when(z + k + 1 <= 3)
        def _():
            z_recv(chunk, k, 1).wait_recv()

    def first(chunk, i, axis):
        ref = land.at[chunk, lax.rem(z + 1 + i, 4), y, x, c, axis]
        return remote(ref, ref, xs.at[chunk, 0, axis, i], xr.at[chunk, 0, axis, i], y_nb if axis else x_nb)

    def first_recv(chunk, i, axis):
        piece = lax.rem(z + 1 + i, 4)
        ref = land.at[chunk, piece, 1 - y, x, c, 1] if axis else land.at[chunk, piece, y, 1 - x, c, 0]
        return remote(ref, ref, xs.at[chunk, 0, axis, i], xr.at[chunk, 0, axis, i], y_nb if axis else x_nb)

    def second(chunk, i, axis):
        piece = lax.rem(z + 1 + i, 4)
        ref = land.at[chunk, piece, :, x, c, 1] if axis else land.at[chunk, piece, y, :, c, 0]
        return remote(ref, ref, xs.at[chunk, 1, axis, i], xr.at[chunk, 1, axis, i], x_nb if axis else y_nb)

    def second_recv(chunk, i, axis):
        piece = lax.rem(z + 1 + i, 4)
        ref = land.at[chunk, piece, :, 1 - x, c, 1] if axis else land.at[chunk, piece, 1 - y, :, c, 0]
        return remote(ref, ref, xs.at[chunk, 1, axis, i], xr.at[chunk, 1, axis, i], x_nb if axis else y_nb)

    def across(chunk, i, core):
        ref = land.at[chunk, lax.rem(z + 1 + i, 4), :, :, core]
        return remote(ref, ref, cs.at[chunk, i], cr.at[chunk, i], c_nb)

    def stage0(chunk):
        for index in range(CHUNKS):
            @pl.when(chunk == index)
            def _():
                for copy in own(index):
                    copy.wait()

        z_start(chunk, 0)

    def stage1(chunk):
        z_wait(chunk, 0)
        z_start(chunk, 1)

    def stage2(chunk):
        z_wait(chunk, 1)
        z_start(chunk, 2)

    def stage3(chunk):
        z_wait(chunk, 2)
        for i in range(3):
            for axis in range(2):
                first(chunk, i, axis).start()

    def stage4(chunk):
        for i in range(3):
            for axis in range(2):
                first_recv(chunk, i, axis).wait_recv()
        for i in range(3):
            for axis in range(2):
                second(chunk, i, axis).start()

    def stage5(chunk):
        for i in range(3):
            for axis in range(2):
                second_recv(chunk, i, axis).wait_recv()
        for i in range(3):
            across(chunk, i, c).start()

    def stage6(chunk):
        for i in range(3):
            across(chunk, i, 1 - c).wait_recv()
        for i in range(3):
            across(chunk, i, c).wait_send()
            for axis in range(2):
                first(chunk, i, axis).wait_send()
                second(chunk, i, axis).wait_send()
        for k in range(3):
            z_each(chunk, k, lambda copy: copy.wait_send())

    stages = [stage0, stage1, stage2, stage3, stage4, stage5, stage6]

    def tick(step):
        for index in reversed(range(len(stages))):
            begun = step - GATHER_OFFSETS[index]
            chunk = begun - jnp.where(begun >= 3, GATHER_DELAY, 0)

            @pl.when((begun >= 0) & ((begun < 3) | (begun >= 3 + GATHER_DELAY)) & (chunk < CHUNKS))
            def _():
                stages[index](chunk)

    results = [
        pltpu.make_async_copy(a, b, os_.at[i])
        for i, (a, b) in enumerate(
            [
                (rows.at[0], home_hbm), (normed, normed_hbm), (buf, buf_hbm), (mine, mine_hbm),
                (level_out, level_hbm), (mixed_low, mixed_hbm), (residual, residual_hbm), (branch, branch_hbm),
            ]
        )
    ]

    rows_start(hidden, 0)
    for k in range(3):
        small_copy(k).start()
    small_land[z] = small[...]

    @pl.loop(0, 4)
    def _(step):
        tick(step)

    for k in range(3):
        small_recv(k).wait_recv()
    for i in range(4):
        full[:, i * shard : (i + 1) * shard] = small_land[i].astype(F32)
    rows_wait(hidden, 0)

    def vector(index):
        return full[index : index + 1, :]

    @pl.loop(0, 4)
    def _(i):
        part = layer_norm(rows[0, i].astype(F32), vector(3), vector(4))
        normed[lanes_of(i), :] = part.astype(BF16)
        tick(4 + i)

    @pl.loop(8, 12)
    def _(step):
        tick(step)

    rows_start(cotangent, 1)
    results[0].start()
    results[1].start()
    for chunk in range(3):
        pltpu.make_async_copy(land.at[chunk], kept.at[chunk], kd.at[chunk]).start()
    tile = 256
    for u in range(3):
        @pl.loop(0, width // tile)
        def _(n):
            cut = lanes_of(n, tile)
            part = matmul(normed[...], flat_rows(land[u, :, :, :, :, :, :, cut]))
            if u != 1:
                part += full[u // 2 : u // 2 + 1, cut]
            qkv[u, :, cut] = part.astype(BF16)

        if u < 2:
            tick(12 + u)

    def send(h):
        return remote(
            qkv.at[:, :, lanes_of((1 - c) * pairs + h)],
            buf.at[:, lanes_of(c, half), lanes_of(h)], es.at[h], er.at[h], c_nb,
        )

    def keep(h):
        return pltpu.make_async_copy(
            qkv.at[:, :, lanes_of(c * pairs + h)], buf.at[:, lanes_of(c, half), lanes_of(h)], ek.at[h]
        )

    def recv(h):
        ref = buf.at[:, lanes_of(1 - c, half), lanes_of(h)]
        return remote(ref, ref, es.at[h], er.at[h], c_nb)

    def send_back(h):
        return remote(
            mine.at[lanes_of(1 - c, half), lanes_of(h)], mixed_low.at[:, lanes_of(c * pairs + h)],
            fs.at[h], fr.at[h], c_nb,
        )

    def keep_back(h):
        return pltpu.make_async_copy(
            mine.at[lanes_of(c, half), lanes_of(h)], mixed_low.at[:, lanes_of(c * pairs + h)], fk.at[h]
        )

    def recv_back(h):
        ref = mixed_low.at[:, lanes_of((1 - c) * pairs + h)]
        return remote(ref, ref, fs.at[h], fr.at[h], c_nb)

    @pl.loop(0, pairs)
    def _(h):
        send(h).start()
        keep(h).start()

    @pl.loop(0, pairs)
    def _(h):
        keep(h).wait()
        recv(h).wait_recv()
        cut = lanes_of(h)

        def put(start, stop, mixed, level):
            level_out[start:stop, cut] = level
            mine[start:stop, cut] = mixed.astype(BF16)

        attend(buf.at[0, :, cut], buf.at[1, :, cut], buf.at[2, :, cut], length, 256, put)
        send_back(h).start()
        keep_back(h).start()
        tick(14 + h)

    @pl.loop(0, pairs)
    def _(h):
        keep_back(h).wait()
        recv_back(h).wait_recv()
        send(h).wait_send()
        send_back(h).wait_send()

    for i in range(2, 6):
        results[i].start()

    act, d_pre, normed2 = qkv.at[0], qkv.at[1], qkv.at[2]

    @pl.loop(0, width // tile)
    def _(n):
        cut = lanes_of(n, tile)
        part = matmul(mixed_low[...], flat_rows(land[3, :, :, :, :, :, :, cut]))
        residual[:, cut] = flat_rows(rows[0, :, :, cut]).astype(F32) + part + full[2:3, cut]

    pltpu.make_async_copy(land.at[3], kept.at[3], kd.at[3]).start()
    tick(18)
    rows_wait(cotangent, 1)

    @pl.loop(0, 4)
    def _(i):
        cut = lanes_of(i)
        normed2[cut, :] = layer_norm(residual[cut, :], vector(6), vector(7)).astype(BF16)
        position = c * half + i * 128 + lax.broadcasted_iota(jnp.int32, (128, 1), 0)
        d_out = jnp.where(position < length, rows[1, i].astype(F32), 0.0)
        branch[cut, :] = d_out.astype(BF16)

    results[6].start()
    results[7].start()

    total[...] = jnp.zeros_like(total)
    dx[...] = jnp.zeros_like(dx)
    turned[...] = normed2[...].T

    def put_up(j, n):
        cut = lanes_of(n, tile)
        return pltpu.make_async_copy(stage_up.at[:, cut], g_up.at[j, :, cut], us.at[n])

    def put_down(j, n):
        cut = lanes_of(n, tile)
        return pltpu.make_async_copy(stage_down.at[cut, :], g_down.at[j, cut, :], ds_.at[n])

    @pl.loop(0, HIDDEN_BLOCKS)
    def _(j):
        up, down = UP + 2 * j, DOWN + 2 * j

        @pl.loop(0, width // tile)
        def _(n):
            cut = lanes_of(n, tile)

            @pl.when(j > 0)
            def _():
                put_up(j, n).wait()
                put_down(j, n).wait()

            pre = matmul(normed2[...], flat_rows(land[up, :, :, :, :, :, :, cut])) + full[pl.ds(8 + j, 1), cut]
            cumulative = 0.5 + 0.5 * lax.erf(pre * (0.5**0.5))
            active = (pre * cumulative).astype(BF16)
            act[:, cut] = active
            slope = cumulative + pre * (jnp.exp(-0.5 * pre * pre) * 0.3989422804014327)
            low = (dot_nt(branch[...], flat_rows(land[down, n])) * slope).astype(BF16)
            d_pre[:, cut] = low
            g_bias[pl.ds(j, 1), cut] = jnp.sum(low.astype(F32), axis=0, keepdims=True)
            stage_down[cut, :] = matmul(active.T, branch[...]).astype(BF16)
            stage_up[:, cut] = matmul(turned[...], low).astype(BF16)
            put_up(j, n).start()
            put_down(j, n).start()

        tick(19 + 2 * j)

        @pl.loop(0, width // tile)
        def _(n):
            cut = lanes_of(n, tile)
            total[:, cut] += matmul(act[...], flat_rows(land[down, :, :, :, :, :, :, cut]))
            dx[:, cut] += dot_nt(d_pre[...], flat_rows(land[up, n]))

        tick(20 + 2 * j)

    output[...] = (residual[...] + total[...] + full[5:6, :]).astype(BF16)
    for n in range(width // tile):
        put_up(0, n).wait()
        put_down(0, n).wait()
    for copy in results:
        copy.wait()
    for chunk in range(4):
        pltpu.make_async_copy(land.at[chunk], kept.at[chunk], kd.at[chunk]).wait()
    for k in range(3):
        small_copy(k).wait_send()


def forward(w_qkv, w_out, w_up, w_down, small, hidden, cotangent, lengths):
    shard, width = w_out.shape
    half = hidden.shape[0] * hidden.shape[1]
    slots, mine = 2 * half, width // 2
    pairs = mine // 128
    piece = (2, 2, 2, 2, shard // 16)
    vm, anywhere = pl.BlockSpec(memory_space=VMEM), pl.BlockSpec(memory_space=pl.ANY)
    shape = jax.ShapeDtypeStruct
    n = CHUNKS
    return pl.pallas_call(
        forward_kernel,
        out_shape=(
            shape((4, 4) + piece + (width,), BF16),
            shape((16, width), F32),
            shape(hidden.shape, BF16),
            shape((half, width), BF16),
            shape((half, width), BF16),
            shape((3, slots, mine), BF16),
            shape((slots, mine), BF16),
            shape((slots, mine), F32),
            shape((half, width), BF16),
            shape((half, width), F32),
            shape((half, width), F32),
            shape((HIDDEN_BLOCKS, width, width), BF16),
            shape((HIDDEN_BLOCKS, width, width), BF16),
            shape((8, width), F32),
            shape((half, width), BF16),
        ),
        in_specs=[anywhere] * 4 + [vm] + [anywhere] * 2 + [pl.BlockSpec(memory_space=pltpu.SMEM)],
        out_specs=(anywhere, vm) + (anywhere,) * 8 + (vm, anywhere, anywhere, vm, vm),
        scratch_shapes=[
            VMEM((2,) + hidden.shape, BF16),
            VMEM((half, width), BF16),
            VMEM((half, width), BF16),
            VMEM((3, slots, mine), BF16),
            VMEM((slots, mine), BF16),
            VMEM((slots, mine), F32),
            VMEM((half, width), BF16),
            VMEM((half, width), F32),
            VMEM((n, 4) + piece + (width,), BF16),
            VMEM((4,) + small.shape, BF16),
            VMEM((3, half, width), BF16),
            VMEM((width, half), BF16),
            VMEM((half, width), F32),
            VMEM((width, width), BF16),
            VMEM((width, width), BF16),
            DMA((n, 4)), DMA((4,)), DMA((3,)), DMA((3,)),
            DMA((n, 2, 3)), DMA((n, 2, 3)),
            DMA((n, 2, 2, 3)), DMA((n, 2, 2, 3)),
            DMA((n, 3)), DMA((n, 3)),
            DMA((2, 4)), DMA((2, 4)),
            DMA((pairs,)), DMA((pairs,)), DMA((pairs,)),
            DMA((pairs,)), DMA((pairs,)), DMA((pairs,)),
            DMA((4,)), DMA((4,)), DMA((8,)),
        ],
        compiler_params=pltpu.CompilerParams(
            collective_id=0, has_side_effects=True, vmem_limit_bytes=VMEM_LIMIT
        ),
        name="forward",
    )(
        w_qkv.reshape(piece + (3 * width,)),
        w_out.reshape(piece + (width,)),
        w_up.reshape(piece + (4 * width,)),
        w_down.reshape((HIDDEN_BLOCKS,) + piece + (width,)),
        small, hidden, cotangent, lengths,
    )


P_OFFSETS = (0, 1, 3, 5, 6, 7, 8, 9, 10, 11)
Q_OFFSETS = (0, 1, 3, 5, 7, 8, 9, 10, 11, 12)
LAST_STEP = 18
N_P, N_Q = 8, 4


def norm_back(x, upstream, gain):
    center = jnp.mean(x, axis=-1, keepdims=True)
    centered = x - center
    scale = lax.rsqrt(jnp.mean(centered * centered, axis=-1, keepdims=True) + EPS)
    hat = centered * scale
    t = upstream * gain
    back = scale * (t - jnp.mean(t, axis=-1, keepdims=True) - hat * jnp.mean(t * hat, axis=-1, keepdims=True))
    return back, jnp.sum(upstream * hat, axis=0, keepdims=True), jnp.sum(upstream, axis=0, keepdims=True)


def backward_kernel(
    kept, full, rows, normed, branch, buf, o_low, levels, mixed_low, residual, dx, g_up, g_down, g_bias, output,
    lengths,
    out, small_out, out_home, grad_home,
    acc, core_in, x_in, y_in, x_in2, y_in2, up_in, down_in, xq_in, yq_in, up_q, down_q, small_in,
    pair, pair_o, pair_l, dm, mine, turned, d_qkv, slot_a, slot_b, keep_f, work_f, d_attn, home_low, weight, stage,
    ls, cs, cr, s1, r1, s2, r2, zs, zr, gl, s3, r3, s4, r4, s5, r5, vs, vr, hs, hr,
    ps, ek, es, er, fk, fs, fr, ms, ws,
):
    d, y, x, c, z = place()
    x_nb, y_nb, c_nb = (d + 2 - 4 * x, z), (d + 4 - 8 * y, z), (d + 1 - 2 * c, z)
    line = [(d, lax.rem(z + k, 4)) for k in (1, 2, 3)]
    width = full.shape[1]
    half = d_attn.shape[0]
    pairs = dm.shape[1] // 128
    length = lengths[d // 4, lax.rem(d // 2, 2)]
    tile = 256

    def local(src, dst, sem):
        return pltpu.make_async_copy(src, dst, sem)

    loads = [
        local(residual, keep_f, ms.at[0]), local(dx, work_f, ms.at[1]), local(branch, slot_b, ms.at[2]),
        local(mixed_low, slot_a, ms.at[3]),
    ]
    for copy in loads:
        copy.start()
    local(kept.at[3], weight, ws).start()
    greet([(lax.rem(d + k, 8), z) for k in range(1, 8)] + line)

    comes, goes = swap_rows(d)

    def row_copy(src, dst, a, i):
        return remote(src(i), dst.at[d // 2], hs.at[a, i], hr.at[a, d // 2], (goes(i), z))

    def row_keep(src, dst, a, i):
        return local(src(i), dst.at[d // 2], hs.at[a, i])

    def row_recv(dst, a, s):
        return remote(dst.at[s], dst.at[s], hs.at[a, s], hr.at[a, s], c_nb)

    def rows_start(src, dst, a):
        for i in range(4):
            @pl.when(goes(i) == d)
            def _():
                row_keep(src, dst, a, i).start()

            @pl.when(goes(i) != d)
            def _():
                row_copy(src, dst, a, i).start()

    def rows_wait(src, dst, a):
        for i in range(4):
            @pl.when(goes(i) == d)
            def _():
                row_keep(src, dst, a, i).wait()

            @pl.when(goes(i) != d)
            def _():
                row_copy(src, dst, a, i).wait_send()

            @pl.when(comes(i) != d)
            def _():
                row_recv(dst, a, i).wait_recv()

    def output_block(i):
        return output.at[i]

    def grad_block(i):
        return home_low.at[i * 128 : (i + 1) * 128, :]

    def load(ref, chunk, slot):
        return local(ref.at[chunk, :, :, :, c], acc.at[slot], ls.at[slot])

    def core_send(ref, slot, into):
        return remote(ref, core_in.at[into], cs.at[slot], cr.at[slot], c_nb)

    def down_send(k):
        return core_send(g_down.at[k, :, :, :, 1 - c], k, k)

    def up_send(k):
        return core_send(g_up.at[k, :, :, :, 1 - c], N_P + k, 5 + k)

    def stage_send(slot, into):
        return core_send(stage, slot, into)

    def core_add(slot, into):
        stage_send(slot, into).wait_recv()
        for piece in range(4):
            acc[slot, piece] += core_in[into, piece]

    def x1(k):
        return remote(acc.at[k, :, :, 1 - x, 0], x_in.at[k], s1.at[k, 0], r1.at[k, 0], x_nb)

    def y1(k):
        return remote(acc.at[k, :, 1 - y, :, 1], y_in.at[k], s1.at[k, 1], r1.at[k, 1], y_nb)

    def y2(k):
        return remote(acc.at[k, :, 1 - y, x, 0], y_in2.at[k], s2.at[k, 0], r2.at[k, 0], y_nb)

    def x2(k):
        return remote(acc.at[k, :, y, 1 - x, 1], x_in2.at[k], s2.at[k, 1], r2.at[k, 1], x_nb)

    def qx1(k):
        return remote(acc.at[N_P + k, z, :, 1 - x, 0], xq_in.at[k, 0:2], s1.at[N_P + k, 0], r1.at[N_P + k, 0], x_nb)

    def qy1(k):
        return remote(acc.at[N_P + k, z, 1 - y, :, 1], yq_in.at[k, 0:2], s1.at[N_P + k, 1], r1.at[N_P + k, 1], y_nb)

    def qy2(k):
        return remote(acc.at[N_P + k, z, 1 - y, x, 0], yq_in.at[k, 2], s2.at[N_P + k, 0], r2.at[N_P + k, 0], y_nb)

    def qx2(k):
        return remote(acc.at[N_P + k, z, y, 1 - x, 1], xq_in.at[k, 2], s2.at[N_P + k, 1], r2.at[N_P + k, 1], x_nb)

    def p_up(k, i):
        return remote(acc.at[k, z + 3 - i, y, x], up_in.at[k, i], zs.at[k, 0, i], zr.at[k, 0, i], (d, z + 1))

    def p_down(k, i):
        return remote(acc.at[k, z - 3 + i, y, x], down_in.at[k, i], zs.at[k, 1, i], zr.at[k, 1, i], (d, z - 1))

    def q_up(k, i):
        return remote(
            acc.at[N_P + k, z + 3 - i], up_q.at[k, i], zs.at[N_P + k, 0, i], zr.at[N_P + k, 0, i], (d, z + 1)
        )

    def q_down(k, i):
        return remote(
            acc.at[N_P + k, z - 3 + i], down_q.at[k, i], zs.at[N_P + k, 1, i], zr.at[N_P + k, 1, i], (d, z - 1)
        )

    def z_each(up, down, k, i, act):
        @pl.when((z < 3) & (z <= i))
        def _():
            act(up(k, i))

        @pl.when((z > 0) & (z >= 3 - i))
        def _():
            act(down(k, i))

    def z_send(up, down, k, i):
        z_each(up, down, k, i, lambda copy: copy.start())

    def z_add(up_ref, down_ref, k, base, i, add_up, add_down):
        @pl.when((z >= 1) & (z - 1 <= i))
        def _():
            ref = up_ref.at[k, i]
            remote(ref, ref, zs.at[base + k, 0, i], zr.at[base + k, 0, i], c_nb).wait_recv()
            add_up(k, i)

        @pl.when((z <= 2) & (z + 1 >= 3 - i))
        def _():
            ref = down_ref.at[k, i]
            remote(ref, ref, zs.at[base + k, 1, i], zr.at[base + k, 1, i], c_nb).wait_recv()
            add_down(k, i)

    def p_add_up(k, i):
        acc[k, z + 2 - i, y, x] += up_in[k, i]

    def p_add_down(k, i):
        acc[k, z - 2 + i, y, x] += down_in[k, i]

    def q_add_up(k, i):
        acc[N_P + k, z + 2 - i] += up_q[k, i]

    def q_add_down(k, i):
        acc[N_P + k, z - 2 + i] += down_q[k, i]

    def g0(k):
        return local(acc.at[k, z, y, x], out.at[k, y, x, c], gl.at[k])

    def g1(k, axis):
        return remote(
            acc.at[k, z, y, x, axis], out.at[k, y, x, c, axis], s3.at[k, axis], r3.at[k, axis],
            y_nb if axis else x_nb,
        )

    def g1_recv(k, axis):
        ref = out.at[k, 1 - y, x, c, 1] if axis else out.at[k, y, 1 - x, c, 0]
        return remote(ref, ref, s3.at[k, axis], r3.at[k, axis], y_nb if axis else x_nb)

    def g2(k, axis):
        ref = out.at[k, :, x, c, 1] if axis else out.at[k, y, :, c, 0]
        return remote(ref, ref, s4.at[k, axis], r4.at[k, axis], x_nb if axis else y_nb)

    def g2_recv(k, axis):
        ref = out.at[k, :, 1 - x, c, 1] if axis else out.at[k, 1 - y, :, c, 0]
        return remote(ref, ref, s4.at[k, axis], r4.at[k, axis], x_nb if axis else y_nb)

    def g3(k, core):
        ref = out.at[k, :, :, core]
        return remote(ref, ref, s5.at[k], r5.at[k], c_nb)

    def spread1(k):
        g0(k).start()
        g1(k, 0).start()
        g1(k, 1).start()

    def spread2(k):
        g0(k).wait()
        for axis in range(2):
            g1_recv(k, axis).wait_recv()
        for axis in range(2):
            g2(k, axis).start()

    def spread3(k):
        for axis in range(2):
            g2_recv(k, axis).wait_recv()
        g3(k, c).start()

    def spread4(k):
        g3(k, 1 - c).wait_recv()
        g3(k, c).wait_send()
        for axis in range(2):
            g1(k, axis).wait_send()
            g2(k, axis).wait_send()

    def p0(k):
        @pl.when(k < 4)
        def _():
            down_send(k).start()
            load(g_down, k, k).start()

    def p1(k):
        @pl.when(k < 4)
        def _():
            load(g_down, k, k).wait()

        core_add(k, jnp.where(k >= 5, k - 5, k))
        x1(k).start()
        y1(k).start()

    def p2(k):
        x1(k).wait_recv()
        y1(k).wait_recv()
        acc[k, :, :, x, 0] += x_in[k]
        acc[k, :, y, :, 1] += y_in[k]
        y2(k).start()
        x2(k).start()

    def p3(k):
        y2(k).wait_recv()
        x2(k).wait_recv()
        acc[k, :, y, x, 0] += y_in2[k]
        acc[k, :, y, x, 1] += x_in2[k]
        z_send(p_up, p_down, k, 0)

    def p4(k):
        z_add(up_in, down_in, k, 0, 0, p_add_up, p_add_down)
        z_send(p_up, p_down, k, 1)

    def p5(k):
        z_add(up_in, down_in, k, 0, 1, p_add_up, p_add_down)
        z_send(p_up, p_down, k, 2)

    def p6(k):
        z_add(up_in, down_in, k, 0, 2, p_add_up, p_add_down)
        spread1(k)

    def p9(k):
        spread4(k)

        @pl.when(k < 4)
        def _():
            down_send(k).wait_send()

        for copy in (x1(k), y1(k), x2(k), y2(k)):
            copy.wait_send()
        for i in range(3):
            z_each(p_up, p_down, k, i, lambda copy: copy.wait_send())

    def q0(k):
        up_send(k).start()
        load(g_up, k, N_P + k).start()

    def q1(k):
        load(g_up, k, N_P + k).wait()
        core_add(N_P + k, 5 + k)
        z_send(q_up, q_down, k, 0)

    def q2(k):
        z_add(up_q, down_q, k, N_P, 0, q_add_up, q_add_down)
        z_send(q_up, q_down, k, 1)

    def q3(k):
        z_add(up_q, down_q, k, N_P, 1, q_add_up, q_add_down)
        z_send(q_up, q_down, k, 2)

    def q4(k):
        z_add(up_q, down_q, k, N_P, 2, q_add_up, q_add_down)
        qx1(k).start()
        qy1(k).start()

    def q5(k):
        qx1(k).wait_recv()
        qy1(k).wait_recv()
        acc[N_P + k, z, :, x, 0] += xq_in[k, 0:2]
        acc[N_P + k, z, y, :, 1] += yq_in[k, 0:2]
        qy2(k).start()
        qx2(k).start()

    def q6(k):
        qy2(k).wait_recv()
        qx2(k).wait_recv()
        acc[N_P + k, z, y, x, 0] += yq_in[k, 2]
        acc[N_P + k, z, y, x, 1] += xq_in[k, 2]
        spread1(N_P + k)

    def q9(k):
        spread4(N_P + k)
        up_send(k).wait_send()
        for copy in (qx1(k), qy1(k), qx2(k), qy2(k)):
            copy.wait_send()
        for i in range(3):
            z_each(q_up, q_down, k, i, lambda copy: copy.wait_send())

    p_stages = [p0, p1, p2, p3, p4, p5, p6, spread2, spread3, p9]
    q_stages = [
        q0, q1, q2, q3, q4, q5, q6, lambda k: spread2(N_P + k), lambda k: spread3(N_P + k), q9,
    ]

    def tick(step):
        step = jnp.asarray(step, jnp.int32)
        for index in reversed(range(10)):
            q_begun = step - Q_OFFSETS[index]

            @pl.when((q_begun == 0) | ((q_begun >= 0) & (q_begun < 2 * N_Q - 1) & (lax.rem(q_begun + 64, 2) == 1)))
            def _():
                q_stages[index]((q_begun + 1) // 2)

            begun = step - P_OFFSETS[index]

            @pl.when((begun >= 0) & (begun < N_P))
            def _():
                p_stages[index](begun)

    tick(0)
    rows_start(output_block, out_home, 0)

    for copy in loads:
        copy.wait()
    small_out[0] = jnp.zeros_like(small_out[0])
    small_out[0, 8:12, :] = g_bias[0:4, :]

    def add_small(index, value):
        small_out[0, index : index + 1, :] += value

    @pl.loop(0, 4)
    def _(i):
        cut = lanes_of(i)
        d_out = slot_b[cut, :].astype(F32)
        back, gain, shift = norm_back(keep_f[cut, :], work_f[cut, :], full[6:7, :])
        d_residual = d_out + back
        keep_f[cut, :] = d_residual
        low = d_residual.astype(BF16)
        d_attn[cut, :] = low
        add_small(2, jnp.sum(low.astype(F32), axis=0, keepdims=True))
        add_small(5, jnp.sum(d_out, axis=0, keepdims=True))
        add_small(6, gain)
        add_small(7, shift)

    tick(1)

    def put_gradient(slot, cut, value):
        value = value.astype(BF16).reshape(4, 2, 2, 2, 2, 16, tile)
        even, odd = value[:, :, :, 0], value[:, :, :, 1]
        first = c == 0
        acc[slot, :, :, :, :, :, cut] = jnp.where(first, even, odd)
        stage[:, :, :, :, :, cut] = jnp.where(first, odd, even)

    for i in range(2):
        d_qkv[0, :, i * half : (i + 1) * half] = slot_a[:, i * half : (i + 1) * half].T

    @pl.loop(0, width // tile)
    def _(n):
        cut = lanes_of(n, tile)
        halves = [matmul(d_qkv[0, :, i * half : (i + 1) * half], d_attn[:, cut]) for i in range(2)]
        put_gradient(4, cut, jnp.concatenate(halves, axis=0))

    stage_send(4, 4).start()
    local(kept.at[3], weight, ws).wait()

    @pl.loop(0, width // tile)
    def _(n):
        cut = lanes_of(n, tile)
        home_low[:, cut] = dot_nt(d_attn[...], flat_rows(weight[n])).astype(BF16)

    local(kept.at[0], weight, ws).start()
    home_rows = local(rows, slot_b, ms.at[2])
    normed_rows = local(normed, slot_a, ms.at[3])
    home_rows.start()
    normed_rows.start()

    def pair_loads(h):
        slot = lax.rem(h, 2)
        cut = lanes_of(h)
        return [
            local(buf.at[:, :, cut], pair.at[slot], ps.at[slot, 0]),
            local(o_low.at[:, cut], pair_o.at[slot], ps.at[slot, 1]),
            local(levels.at[:, cut], pair_l.at[slot], ps.at[slot, 2]),
        ]

    def send(h):
        return remote(
            home_low.at[:, lanes_of((1 - c) * pairs + h)], dm.at[lanes_of(c, half), lanes_of(h)],
            es.at[h], er.at[h], c_nb,
        )

    def keep(h):
        return local(home_low.at[:, lanes_of(c * pairs + h)], dm.at[lanes_of(c, half), lanes_of(h)], ek.at[h])

    def recv(h):
        ref = dm.at[lanes_of(1 - c, half), lanes_of(h)]
        return remote(ref, ref, es.at[h], er.at[h], c_nb)

    def send_back(h):
        return remote(
            mine.at[lax.rem(h, 2), :, lanes_of(1 - c, half), :], d_qkv.at[:, :, lanes_of(c * pairs + h)],
            fs.at[h], fr.at[h], c_nb,
        )

    def keep_back(h):
        return local(
            mine.at[lax.rem(h, 2), :, lanes_of(c, half), :], d_qkv.at[:, :, lanes_of(c * pairs + h)], fk.at[h]
        )

    def recv_back(h):
        ref = d_qkv.at[:, :, lanes_of((1 - c) * pairs + h)]
        return remote(ref, ref, fs.at[h], fr.at[h], c_nb)

    for copy in pair_loads(0):
        copy.start()

    @pl.loop(0, pairs)
    def _(h):
        send(h).start()
        keep(h).start()

    tick(2)

    @pl.loop(0, pairs)
    def _(h):
        for copy in pair_loads(h):
            copy.wait()

        @pl.when(h + 1 < pairs)
        def _():
            for copy in pair_loads(h + 1):
                copy.start()

        keep(h).wait()
        recv(h).wait_recv()

        @pl.when(h >= 2)
        def _():
            send_back(h - 2).wait_send()
            keep_back(h - 2).wait()

        turned[...] = jnp.zeros_like(turned)
        slot = lax.rem(h, 2)

        def put_query(start, stop, value):
            mine[slot, 0, start:stop, :] = value.astype(BF16)

        def put_key(start, stop, d_key, d_value):
            turned[0, :, :stop] += d_key
            turned[1, :, :stop] += d_value

        attend_back(
            pair.at[slot, 0], pair.at[slot, 1], pair.at[slot, 2], pair_o.at[slot], pair_l.at[slot],
            dm.at[:, lanes_of(h)], length, 256, put_query, put_key,
        )
        mine[slot, 1] = turned[0].T.astype(BF16)
        mine[slot, 2] = turned[1].T.astype(BF16)
        send_back(h).start()
        keep_back(h).start()
        tick(jnp.where(lax.rem(h, 2) == 1, 3 + h // 2, -1000))

    @pl.loop(0, pairs)
    def _(h):
        recv_back(h).wait_recv()
        send(h).wait_send()

    for h in range(pairs - 2, pairs):
        send_back(h).wait_send()
        keep_back(h).wait()
    home_rows.wait()
    normed_rows.wait()

    dm[...] = slot_a[...].T
    for u in range(3):
        stage_send(4 + u, 4 if u == 0 else u - 1).wait_send()

        @pl.loop(0, width // tile)
        def _(n):
            cut = lanes_of(n, tile)
            put_gradient(5 + u, cut, matmul(dm[...], d_qkv[u, :, cut]))

        stage_send(5 + u, u).start()
        local(kept.at[u], weight, ws).wait()

        @pl.loop(0, width // tile)
        def _(n):
            cut = lanes_of(n, tile)
            part = dot_nt(d_qkv[u], flat_rows(weight[n]))
            work_f[:, cut] = part if u == 0 else work_f[:, cut] + part

        if u < 2:
            local(kept.at[u + 1], weight, ws).start()
        if u != 1:
            add_small(u // 2, jnp.sum(d_qkv[u].astype(F32), axis=0, keepdims=True))
        tick(5 + u)

    @pl.loop(0, 4)
    def _(i):
        cut = lanes_of(i)
        back, gain, shift = norm_back(slot_b[cut, :].astype(F32), work_f[cut, :], full[3:4, :])
        home_low[cut, :] = (keep_f[cut, :] + back).astype(BF16)
        add_small(3, gain)
        add_small(4, shift)

    rows_start(grad_block, grad_home, 1)

    def vector_copy(step):
        nb = (c_nb, x_nb, y_nb)[step]
        return remote(small_out.at[step], small_in.at[step], vs.at[step], vr.at[step], nb)

    for step in range(3):
        vector_copy(step).start()
        tick(8 + step)
        vector_copy(step).wait()
        small_out[step + 1] = small_out[step] + small_in[step]
    copies = [remote(small_out.at[3], small_in.at[3 + k], vs.at[3 + k], vr.at[3 + k], line[k]) for k in range(3)]
    for copy in copies:
        copy.start()

    @pl.loop(11, LAST_STEP + 1)
    def _(step):
        tick(step)

    for copy in copies:
        copy.wait()
    small_out[4] = small_out[3] + small_in[3] + small_in[4] + small_in[5]
    stage_send(7, 2).wait_send()
    rows_wait(output_block, out_home, 0)
    rows_wait(grad_block, grad_home, 1)


def backward(
    kept, full, rows, normed, branch, buf, o_low, levels, mixed_low, residual, dx, g_up, g_down, g_bias, output, lengths
):
    half, width = normed.shape
    slots, lanes = o_low.shape
    pairs = lanes // 128
    piece, n = 16, N_P + N_Q
    vm, anywhere = pl.BlockSpec(memory_space=VMEM), pl.BlockSpec(memory_space=pl.ANY)
    shape = jax.ShapeDtypeStruct
    block = (4, 2, 2, 2, 2, piece, width)
    home = (4, half // 4, width)
    vectors = (16, width)
    out, small_out, out_home, grad_home = pl.pallas_call(
        backward_kernel,
        out_shape=(
            shape((n, 2, 2, 2, 2, piece, width), BF16),
            shape((5,) + vectors, F32),
            shape(home, BF16),
            shape(home, BF16),
        ),
        in_specs=[anywhere, vm] + [anywhere] * 11 + [vm, anywhere, pl.BlockSpec(memory_space=pltpu.SMEM)],
        out_specs=(anywhere, vm, anywhere, anywhere),
        scratch_shapes=[
            VMEM((n, 4, 2, 2, 2, piece, width), BF16),
            VMEM((9, 4, 2, 2, 2, piece, width), BF16),
            VMEM((N_P, 4, 2, piece, width), BF16),
            VMEM((N_P, 4, 2, piece, width), BF16),
            VMEM((N_P, 4, piece, width), BF16),
            VMEM((N_P, 4, piece, width), BF16),
            VMEM((N_P, 3, 2, piece, width), BF16),
            VMEM((N_P, 3, 2, piece, width), BF16),
            VMEM((N_Q, 3, piece, width), BF16),
            VMEM((N_Q, 3, piece, width), BF16),
            VMEM((N_Q, 3, 2, 2, 2, piece, width), BF16),
            VMEM((N_Q, 3, 2, 2, 2, piece, width), BF16),
            VMEM((6,) + vectors, F32),
            VMEM((2, 3, slots, 128), BF16),
            VMEM((2, slots, 128), BF16),
            VMEM((2, slots, 128), F32),
            VMEM((slots, lanes), BF16),
            VMEM((2, 3, slots, 128), BF16),
            VMEM((2, 128, slots), F32),
            VMEM((3, half, width), BF16),
            VMEM((half, width), BF16),
            VMEM((half, width), BF16),
            VMEM((half, width), F32),
            VMEM((half, width), F32),
            VMEM((half, width), BF16),
            VMEM((half, width), BF16),
            VMEM(block, BF16),
            VMEM((4, 2, 2, 2, piece, width), BF16),
            DMA((n,)), DMA((n,)), DMA((n,)),
            DMA((n, 2)), DMA((n, 2)), DMA((n, 2)), DMA((n, 2)),
            DMA((n, 2, 3)), DMA((n, 2, 3)), DMA((n,)),
            DMA((n, 2)), DMA((n, 2)), DMA((n, 2)), DMA((n, 2)),
            DMA((n,)), DMA((n,)), DMA((6,)), DMA((6,)),
            DMA((2, 4)), DMA((2, 4)),
            DMA((2, 3)),
            DMA((pairs,)), DMA((pairs,)), DMA((pairs,)),
            DMA((pairs,)), DMA((pairs,)), DMA((pairs,)),
            DMA((4,)), DMA,
        ],
        compiler_params=pltpu.CompilerParams(
            collective_id=1, has_side_effects=True, vmem_limit_bytes=VMEM_LIMIT
        ),
        name="backward",
    )(
        kept, full, rows.reshape(half, width), normed, branch, buf, o_low, levels, mixed_low, residual, dx,
        g_up.reshape((N_Q,) + block), g_down.reshape((4,) + block), g_bias, output.reshape(home), lengths,
    )
    return out.reshape(n, 16 * piece, width), small_out[4], out_home, grad_home


def feed_kernel(x, d_out, w_up, w_down, bias, y, dx, g_up, g_down, g_bias, x_turned, act, d_pre):
    tile = 256
    hidden = w_up.shape[2]

    @pl.when(pl.program_id(0) == 0)
    def _():
        y[...] = jnp.zeros_like(y)
        dx[...] = jnp.zeros_like(dx)
        x_turned[...] = x[...].T

    @pl.loop(0, hidden // tile)
    def _(n):
        cut = pl.ds(pl.multiple_of(n * tile, tile), tile)
        pre = matmul(x[...], w_up[0, :, cut]) + bias[0, :, cut].astype(F32)
        cumulative = 0.5 + 0.5 * lax.erf(pre * (0.5**0.5))
        active = (pre * cumulative).astype(BF16)
        act[:, cut] = active
        slope = cumulative + pre * (jnp.exp(-0.5 * pre * pre) * 0.3989422804014327)
        back = dot_nt(d_out[...], w_down[0, cut, :]) * slope
        low = back.astype(BF16)
        d_pre[:, cut] = low
        g_bias[0, :, cut] = jnp.sum(low.astype(F32), axis=0, keepdims=True)
        g_down[0, cut, :] = matmul(active.T, d_out[...]).astype(BF16)
        g_up[0, :, cut] = matmul(x_turned[...], low).astype(BF16)

    @pl.loop(0, y.shape[1] // tile)
    def _(n):
        cut = pl.ds(pl.multiple_of(n * tile, tile), tile)
        y[:, cut] += matmul(act[...], w_down[0, :, cut])
        dx[:, cut] += dot_nt(d_pre[...], w_up[0, cut, :])


def feed_forward(x, d_out, weights, bias, first_up, first_down, blocks):
    rows, width = x.shape
    hidden = weights.shape[2]
    whole = pl.BlockSpec((rows, width), lambda j: (0, 0))
    return pl.pallas_call(
        feed_kernel,
        grid=(blocks,),
        out_shape=(
            jax.ShapeDtypeStruct((rows, width), F32),
            jax.ShapeDtypeStruct((rows, width), F32),
            jax.ShapeDtypeStruct((blocks, width, hidden), BF16),
            jax.ShapeDtypeStruct((blocks, hidden, width), BF16),
            jax.ShapeDtypeStruct((blocks, 1, hidden), F32),
        ),
        in_specs=[
            whole,
            whole,
            pl.BlockSpec((1, width, hidden), lambda j: (first_up + j, 0, 0)),
            pl.BlockSpec((1, hidden, width), lambda j: (first_down + j, 0, 0)),
            pl.BlockSpec((1, 1, hidden), lambda j: (j, 0, 0)),
        ],
        out_specs=(
            whole,
            whole,
            pl.BlockSpec((1, width, hidden), lambda j: (j, 0, 0)),
            pl.BlockSpec((1, hidden, width), lambda j: (j, 0, 0)),
            pl.BlockSpec((1, 1, hidden), lambda j: (j, 0, 0)),
        ),
        scratch_shapes=[VMEM((width, rows), BF16), VMEM((rows, hidden), BF16), VMEM((rows, hidden), BF16)],
        compiler_params=pltpu.CompilerParams(
            dimension_semantics=("arbitrary",), vmem_limit_bytes=VMEM_LIMIT
        ),
        cost_estimate=pl.CostEstimate(
            flops=12 * blocks * rows * width * hidden,
            bytes_accessed=8 * blocks * width * hidden + 12 * rows * width,
            transcendentals=2 * blocks * rows * hidden,
        ),
        name="feed_forward",
    )(x, d_out, weights, weights, bias)


def finish_kernel(sums, qkv, out, up, down):
    width = out.shape[1]
    shard = width // 4
    out[...] = sums[4].astype(F32)
    for i in range(3):
        qkv[:, i * width : (i + 1) * width] = sums[5 + i].astype(F32)
    for j in range(4):
        down[j] = sums[j].astype(F32)
        value = sums[8 + j].astype(F32)
        for i in range(4):
            low = i * width + j * shard
            up[:, low : low + shard] = value[:, i * shard : (i + 1) * shard]


def finish(sums):
    n, rows, width = sums.shape
    tile = 32
    qkv, out, up, down = pl.pallas_call(
        finish_kernel,
        grid=(rows // tile,),
        out_shape=(
            jax.ShapeDtypeStruct((rows, 3 * width), F32),
            jax.ShapeDtypeStruct((rows, width), F32),
            jax.ShapeDtypeStruct((rows, 4 * width), F32),
            jax.ShapeDtypeStruct((4, rows, width), F32),
        ),
        in_specs=[pl.BlockSpec((n, tile, width), lambda i: (0, i, 0))],
        out_specs=(
            pl.BlockSpec((tile, 3 * width), lambda i: (i, 0)),
            pl.BlockSpec((tile, width), lambda i: (i, 0)),
            pl.BlockSpec((tile, 4 * width), lambda i: (i, 0)),
            pl.BlockSpec((4, tile, width), lambda i: (0, i, 0)),
        ),
        compiler_params=pltpu.CompilerParams(dimension_semantics=("arbitrary",), vmem_limit_bytes=32 * 1024 * 1024),
        name="finish",
    )(sums)
    return qkv, out, up, down.reshape(4 * rows, width)


def any_finish(sums):
    shard, width = sums.shape[1:]
    shards, blocks = width // shard, (sums.shape[0] - 4) // 2
    sums = sums.astype(F32)
    up = jnp.transpose(sums[4 : 4 + blocks].reshape(blocks, shard, shards, shard), (1, 2, 0, 3))
    return (
        jnp.transpose(sums[:3], (1, 0, 2)).reshape(shard, 3 * width),
        sums[3],
        up.reshape(shard, blocks * width),
        sums[4 + blocks :].reshape(blocks * shard, width),
    )


def any_gather(w_qkv, w_out, w_up, w_down, small):
    shard, width = w_out.shape
    shards, blocks = width // shard, w_up.shape[1] // width
    up_parts = jnp.transpose(w_up.reshape(shard, shards, blocks, shard), (2, 0, 1, 3)).reshape(blocks, shard, width)
    packed = jnp.concatenate(
        [
            jnp.transpose(w_qkv.reshape(shard, 3, width), (1, 0, 2)),
            w_out[None],
            up_parts,
            w_down.reshape(blocks, shard, width),
        ],
        axis=0,
    )
    return (
        lax.all_gather(packed, "fsdp", axis=1, tiled=True),
        lax.all_gather(small, "fsdp", axis=0, tiled=False),
    )


def any_reduce(parts, small):
    out = []
    for part in parts:
        mine = lax.psum_scatter(part, "fsdp", scatter_dimension=1, tiled=True)
        out.append(lax.psum(mine, "ctx"))
    return jnp.concatenate(out, axis=0), lax.psum(small, ("ctx", "fsdp"))


def any_forward(qkv, lengths):
    count = lengths.shape[0]
    qkv = qkv.reshape(3, count, -1, qkv.shape[2])
    wide = lax.all_to_all(qkv, "ctx", split_axis=3, concat_axis=2, tiled=True)
    wide = jnp.swapaxes(wide, 0, 1)

    def one(item):
        rows, length = item
        mixed, levels = [], []

        def put(start, stop, part, level):
            mixed.append(part)
            levels.append(level)

        attend(rows[0], rows[1], rows[2], length, rows.shape[1], put)
        return mixed[0], levels[0]

    mixed, levels = lax.map(one, (wide, lengths))
    low = lax.all_to_all(mixed.astype(BF16), "ctx", split_axis=1, concat_axis=2, tiled=True)
    return low.reshape(-1, low.shape[2]), wide, mixed, levels


def any_backward(dm_home, wide, mixed, levels, lengths):
    dm_home = dm_home.reshape(lengths.shape[0], -1, dm_home.shape[1])
    dm = lax.all_to_all(dm_home, "ctx", split_axis=2, concat_axis=1, tiled=True)

    def one(item):
        rows, part, level, upstream, length = item
        found = {}

        def put_query(start, stop, value):
            found[0] = value.astype(BF16)

        def put_key(start, stop, d_key, d_value):
            found[1], found[2] = d_key.T.astype(BF16), d_value.T.astype(BF16)

        attend_back(
            rows[0], rows[1], rows[2], part, level, upstream, length, rows.shape[1], put_query, put_key
        )
        return jnp.stack([found[0], found[1], found[2]])

    out = lax.map(one, (wide, mixed, levels, dm, lengths))
    out = lax.all_to_all(out, "ctx", split_axis=2, concat_axis=3, tiled=True)
    out = jnp.swapaxes(out, 0, 1)
    return out.reshape(3, -1, out.shape[3])


def any_layer(w_qkv, w_out, w_up, w_down, small, hidden_in, cotangent, flat_lengths):
    batch, seqs, slots, width = hidden_in.shape
    rows = batch * seqs * slots
    blocks = w_up.shape[1] // width
    weights, small_all = any_gather(w_qkv, w_out, w_up, w_down, small)
    position = lax.axis_index("ctx") * slots + jnp.arange(slots, dtype=jnp.int32)
    filled = (position[None, :] < flat_lengths[:, None]).astype(F32)
    small_all = jnp.transpose(small_all, (1, 0, 2)).reshape(16, width)
    full = small_all.astype(F32)
    full_q, full_v, full_bias_out, gain_one, shift_one, full_bias_down, gain_two, shift_two = [
        full[i] for i in range(8)
    ]
    full_up = small_all[8 : 8 + blocks].reshape(blocks, 1, width)
    flat_in = hidden_in.reshape(rows, width).astype(F32)
    normed = layer_norm(flat_in, gain_one, shift_one).astype(BF16)
    queries = (matmul(normed, weights[0]) + full_q).astype(BF16)
    key_rows = matmul(normed, weights[1]).astype(BF16)
    value_rows = (matmul(normed, weights[2]) + full_v).astype(BF16)
    qkv = jnp.stack([queries, key_rows, value_rows])
    mixed_low, wide, mixed, levels = any_forward(qkv, flat_lengths)
    residual = flat_in + matmul(mixed_low, weights[3]) + full_bias_out
    normed2 = layer_norm(residual, gain_two, shift_two).astype(BF16)
    d_out = cotangent.reshape(rows, width).astype(F32) * filled.reshape(rows, 1)
    fed, d_normed2, grad_up, grad_down, grad_bias_up = feed_forward(
        normed2, d_out.astype(BF16), weights, full_up, 4, 4 + blocks, blocks
    )
    output = (residual + fed + full_bias_down).astype(BF16)
    norm_pull_two = jax.vjp(layer_norm, residual, gain_two, shift_two)[1]
    d_resid_norm, grad_ln2_gain, grad_ln2_bias = norm_pull_two(d_normed2)
    d_residual = d_out + d_resid_norm
    d_attn = d_residual.astype(BF16)
    grad_out = dot_tn(mixed_low, d_attn).astype(BF16)
    d_mixed = dot_nt(d_attn, weights[3]).astype(BF16)
    d_qkv = any_backward(d_mixed, wide, mixed, levels, flat_lengths)
    grad_qkv = jnp.stack([dot_tn(normed, d_qkv[i]).astype(BF16) for i in range(3)])
    d_normed = sum(dot_nt(d_qkv[i], weights[i]) for i in range(3))
    norm_pull_one = jax.vjp(layer_norm, flat_in, gain_one, shift_one)[1]
    d_input_norm, grad_ln1_gain, grad_ln1_bias = norm_pull_one(d_normed)
    small_grads = jnp.stack(
        [
            rows_sum(d_qkv[0]),
            rows_sum(d_qkv[2]),
            rows_sum(d_attn),
            grad_ln1_gain,
            grad_ln1_bias,
            jnp.sum(d_out, axis=0),
            grad_ln2_gain,
            grad_ln2_bias,
        ]
        + [grad_bias_up[j, 0] for j in range(blocks)]
        + [jnp.zeros((width,), F32)] * (8 - blocks)
    )
    return output, d_residual + d_input_norm, [grad_qkv, grad_out[None], grad_up, grad_down], small_grads


def body(
    routed,
    hidden_in,
    lengths,
    cotangent,
    w_qkv,
    bias_q,
    bias_v,
    w_out,
    bias_out,
    ln1_gain,
    ln1_bias,
    w_up,
    bias_up,
    w_down,
    bias_down,
    ln2_gain,
    ln2_bias,
):
    batch, seqs, slots, width = hidden_in.shape
    count = batch * seqs
    rows = count * slots
    shard = w_qkv.shape[0]
    blocks = w_up.shape[1] // width
    vectors = [bias_q, bias_v, bias_out, ln1_gain, ln1_bias, bias_down, ln2_gain, ln2_bias]
    vectors += [bias_up[j * shard : (j + 1) * shard] for j in range(blocks)]
    which = lax.broadcasted_iota(jnp.int32, (16, shard), 0)
    small = jnp.zeros((16, shard), BF16)
    for i, vector in enumerate(vectors):
        small = jnp.where(which == i, vector[None, :], small)
    flat_lengths = lengths.reshape(count)
    if routed:
        *kept, output = forward(
            w_qkv, w_out, w_up, w_down, small,
            hidden_in.reshape(count, slots, width), cotangent.reshape(count, slots, width), lengths,
        )
        sums, small_sums, output, grad_hidden = backward(*kept, output, lengths)
        grad_hidden = grad_hidden.astype(F32)
        out_qkv, out_out, out_up, out_down = finish(sums)
    else:
        output, grad_hidden, parts, small_grads = any_layer(
            w_qkv, w_out, w_up, w_down, small, hidden_in, cotangent, flat_lengths
        )
        sums, small_sums = any_reduce(parts, small_grads)
        out_qkv, out_out, out_up, out_down = any_finish(sums)
    mine = lax.dynamic_slice_in_dim(small_sums, lax.axis_index("fsdp") * shard, shard, 1)
    return (
        output.reshape(hidden_in.shape),
        grad_hidden.reshape(hidden_in.shape),
        out_qkv,
        mine[0],
        mine[1],
        out_out,
        mine[2],
        mine[3],
        mine[4],
        out_up,
        mine[8 : 8 + blocks].reshape(blocks * shard),
        out_down,
        mine[5],
        mine[6],
        mine[7],
    )


def solution(mesh):
    row, vector, slot = P("fsdp", None), P("fsdp"), P(None, "fsdp", "ctx", None)
    routed = dict(mesh.shape) == {"ctx": 8, "fsdp": 4}
    return jax.shard_map(
        functools.partial(body, routed),
        mesh=mesh,
        in_specs=(
            slot, P(None, "fsdp"), slot, row, vector, vector, row, vector, vector, vector, row, vector, row, vector,
            vector, vector,
        ),
        out_specs=(
            slot, slot, row, vector, vector, row, vector, vector, vector, row, vector, row, vector, vector, vector,
        ),
        check_vma=False,
    )
```
